32 devices in a mesh: dp: 2 (over core), row: 4 (over y, x), col: 4 (over z).
Axes of the slice: x: 2, y: 2, z: 4, core: 2. Of those that a mesh axis runs over, the one named last changes fastest.
Arguments:
- inputs: bfloat16 [8192, 512], P('dp', ('row', 'col')), may hold values from -6 to 6
- memory: bfloat16 [2048, 512], P('dp', ('row', 'col')), may hold values from -6 to 6
- teacher: bfloat16 [8192, 512], P('dp', ('row', 'col')), may hold values from -6 to 6
- segment_ids: int32 [8192], P('dp'), may hold values from 0 to 12, as said below
- parent_ids: int32 [8192], P('dp'), may hold values from -1 to 10, as said below
- valid_length: int32 [2], P('dp'), may hold values from 1024 to 4096
- query_weight: bfloat16 [512, 512], P('row', 'col'), may hold values from -0.25 to 0.25
- query_bias: bfloat16 [512], P('col'), may hold values from -3 to 3
- key_weight: bfloat16 [512, 512], P('row', 'col'), may hold values from -0.25 to 0.25
- value_weight: bfloat16 [512, 512], P('row', 'col'), may hold values from -0.25 to 0.25
- value_bias: bfloat16 [512], P('col'), may hold values from -3 to 3
- proj_weight: bfloat16 [512, 512], P('col', 'row'), may hold values from -1 to 1
- proj_bias: bfloat16 [512], P('row'), may hold values from -3 to 3
- cross_query_weight: bfloat16 [512, 512], P('row', 'col'), may hold values from -0.25 to 0.25
- cross_query_bias: bfloat16 [512], P('col'), may hold values from -3 to 3
- cross_key_weight: bfloat16 [512, 512], P('row', 'col'), may hold values from -0.25 to 0.25
- cross_value_weight: bfloat16 [512, 512], P('row', 'col'), may hold values from -0.25 to 0.25
- cross_value_bias: bfloat16 [512], P('col'), may hold values from -3 to 3
- cross_proj_weight: bfloat16 [512, 512], P('col', 'row'), may hold values from -1 to 1
- cross_proj_bias: bfloat16 [512], P('row'), may hold values from -3 to 3
- up_weight: bfloat16 [512, 2048], P('row', 'col'), may hold values from -0.25 to 0.25
- up_bias: bfloat16 [2048], P('col'), may hold values from -3 to 3
- down_weight: bfloat16 [2048, 512], P('col', 'row'), may hold values from -0.125 to 0.125
- down_bias: bfloat16 [512], P('row'), may hold values from -3 to 3
Outputs:
- output: bfloat16 [8192, 512], P('dp', ('row', 'col'))
- mean_loss: float32 [], replicated
- grad_input: float32 [8192, 512], P('dp', ('row', 'col'))
- grad_memory: float32 [2048, 512], P('dp', ('row', 'col'))
- grad_query_weight: float32 [512, 512], P('row', 'col')
- grad_query_bias: float32 [512], P('col')
- grad_key_weight: float32 [512, 512], P('row', 'col')
- grad_value_weight: float32 [512, 512], P('row', 'col')
- grad_value_bias: float32 [512], P('col')
- grad_proj_weight: float32 [512, 512], P('col', 'row')
- grad_proj_bias: float32 [512], P('row')
- grad_cross_query_weight: float32 [512, 512], P('row', 'col')
- grad_cross_query_bias: float32 [512], P('col')
- grad_cross_key_weight: float32 [512, 512], P('row', 'col')
- grad_cross_value_weight: float32 [512, 512], P('row', 'col')
- grad_cross_value_bias: float32 [512], P('col')
- grad_cross_proj_weight: float32 [512, 512], P('col', 'row')
- grad_cross_proj_bias: float32 [512], P('row')
- grad_up_weight: float32 [512, 2048], P('row', 'col')
- grad_up_bias: float32 [2048], P('col')
- grad_down_weight: float32 [2048, 512], P('col', 'row')
- grad_down_bias: float32 [512], P('row')
The draws below stay inside these ranges and needn't reach their ends.
Inputs may be any that keep to these rules, and one draw needn't show every extreme that they name: `segment_ids`: within each tree of 4096 positions the segment ids never fall; 0 is the trunk, then four groups follow, each a branch and its two leaves (ids 1 to 12 in that order); every segment has one position or more. `parent_ids`: the parent segment of the token's segment: -1 in the trunk, 0 in a branch, the branch's id in a leaf.
All inputs are finite; a program needn't handle non-finite values.
Results may differ from the reference program's by a relative error of at most 0.03.
The reference program's roundings to bfloat16 on the way (of `attention`, `cross_out` and `active`) count: a program that leaves them out, or rounds other values in their place, can miss the bound.
Values may be sent and summed in bfloat16 or wider, within the bound.
A program may use at most 192 MiB of HBM per device.

```python
import jax
import jax.numpy as jnp
from jax import lax

D = 512
HEADS = 8
HEAD_DIM = 64
FF = 2048
TREE = 4096
TOKENS = 8192
MEM_ROWS = 2048


def tree_segments(key):
    tree_count = TOKENS // TREE
    trunk_key, split_key = jax.random.split(jax.random.fold_in(key, 11))
    trunk = jax.random.randint(trunk_key, (tree_count, 1), TREE * 3 // 8, TREE * 5 // 8 + 1)
    shares = jax.random.randint(split_key, (tree_count, 12), 1, 4)
    running = jnp.cumsum(shares, axis=1)
    ends = trunk + (TREE - trunk) * running // running[:, 11:12]
    bounds = jnp.concatenate([trunk, ends], axis=1)
    positions = jnp.arange(TREE, dtype=jnp.int32)
    return jnp.sum((positions[None, :, None] >= bounds[:, None, :]).astype(jnp.int32), axis=2)


def draw_segment_ids(key, part):
    return tree_segments(key).reshape(-1).astype(jnp.int32)


def draw_parent_ids(key, part):
    segment = tree_segments(key)
    offset = segment - 1
    group_index = offset // 3
    slot_index = offset - 3 * group_index
    parent = jnp.where(segment == 0, -1, jnp.where(slot_index == 0, 0, 1 + 3 * group_index))
    return parent.reshape(-1).astype(jnp.int32)


def draw_valid_length(key, part):
    tree_count = TOKENS // TREE
    index = jnp.arange(tree_count, dtype=jnp.int32)
    low_end = TREE // 4 + TREE // 16
    base_length = low_end + index * (TREE - low_end) // max(tree_count - 1, 1)
    jitter = jax.random.randint(jax.random.fold_in(key, 23), (tree_count,), 0, TREE // 16 + 1)
    return (base_length - jitter).astype(jnp.int32)


def steps_of(stream_key, dims, cuts, least, top_value):
    def one(position, parts):
        heights = jax.random.uniform(jax.random.fold_in(jax.random.fold_in(stream_key, 6), position), (parts,), jnp.float32, least / len(cuts), top_value / len(cuts))
        return jnp.repeat(jnp.exp(heights), dims[position] // parts).reshape((-1,) + (1,) * (len(dims) - position - 1))

    level = one(*cuts[0])
    for cut in cuts[1:]:
        level = level * one(*cut)
    return level


def bell_draw(key, shape, spread, reach, cuts=(), held_as=jnp.bfloat16):
    entries = jax.random.normal(key, shape, jnp.float32) * spread
    if len(cuts) > 0:
        entries = steps_of(key, shape, cuts, -0.22, 0.18) * entries
    return jnp.clip(entries, min=-reach, max=reach).astype(held_as)


def setup_inputs(seed: int = 0) -> dict:
    key_of = jax.random.split(jax.random.key(seed), 25)
    inputs = bell_draw(key_of[0], (TOKENS, D), 1.0, 6.0, ((0, 2), (1, 16)))
    memory = bell_draw(key_of[1], (MEM_ROWS, D), 1.0, 6.0, ((0, 2), (1, 16)))
    teacher = bell_draw(key_of[2], (TOKENS, D), 1.0, 6.0, ((0, 2), (1, 16)))
    segment_ids = draw_segment_ids(jax.random.fold_in(key_of[24], 71), 0)
    parent_ids = draw_parent_ids(jax.random.fold_in(key_of[24], 71), 0)
    valid_length = draw_valid_length(jax.random.fold_in(key_of[24], 71), 0)
    query_weight = bell_draw(key_of[6], (D, D), D ** -0.5, 0.25, ((0, 4), (1, 4)))
    query_bias = bell_draw(key_of[7], (D,), 0.5, 3.0, ((0, 4),))
    key_weight = bell_draw(key_of[8], (D, D), D ** -0.5, 0.25, ((0, 4), (1, 4)))
    value_weight = bell_draw(key_of[9], (D, D), D ** -0.5, 0.25, ((0, 4), (1, 4)))
    value_bias = bell_draw(key_of[10], (D,), 0.5, 3.0, ((0, 4),))
    proj_weight = bell_draw(key_of[11], (D, D), (max(D // 16, 1)) ** -0.5, 1.0, ((0, 4), (1, 4)))
    proj_bias = bell_draw(key_of[12], (D,), 0.5, 3.0, ((0, 4),))
    cross_query_weight = bell_draw(key_of[13], (D, D), D ** -0.5, 0.25, ((0, 4), (1, 4)))
    cross_query_bias = bell_draw(key_of[14], (D,), 0.5, 3.0, ((0, 4),))
    cross_key_weight = bell_draw(key_of[15], (D, D), D ** -0.5, 0.25, ((0, 4), (1, 4)))
    cross_value_weight = bell_draw(key_of[16], (D, D), D ** -0.5, 0.25, ((0, 4), (1, 4)))
    cross_value_bias = bell_draw(key_of[17], (D,), 0.5, 3.0, ((0, 4),))
    cross_proj_weight = bell_draw(key_of[18], (D, D), (max(D // 16, 1)) ** -0.5, 1.0, ((0, 4), (1, 4)))
    cross_proj_bias = bell_draw(key_of[19], (D,), 0.5, 3.0, ((0, 4),))
    up_weight = bell_draw(key_of[20], (D, FF), D ** -0.5, 0.25, ((0, 4), (1, 4)))
    up_bias = bell_draw(key_of[21], (FF,), 0.5, 3.0, ((0, 4),))
    down_weight = bell_draw(key_of[22], (FF, D), FF ** -0.5, 0.125, ((0, 4), (1, 4)))
    down_bias = bell_draw(key_of[23], (D,), 0.5, 3.0, ((0, 4),))
    return {"inputs": inputs, "memory": memory, "teacher": teacher, "segment_ids": segment_ids, "parent_ids": parent_ids, "valid_length": valid_length, "query_weight": query_weight, "query_bias": query_bias, "key_weight": key_weight, "value_weight": value_weight, "value_bias": value_bias, "proj_weight": proj_weight, "proj_bias": proj_bias, "cross_query_weight": cross_query_weight, "cross_query_bias": cross_query_bias, "cross_key_weight": cross_key_weight, "cross_value_weight": cross_value_weight, "cross_value_bias": cross_value_bias, "cross_proj_weight": cross_proj_weight, "cross_proj_bias": cross_proj_bias, "up_weight": up_weight, "up_bias": up_bias, "down_weight": down_weight, "down_bias": down_bias}


@jax.custom_vjp
def low(v):
    return lax.optimization_barrier(v.astype(jnp.bfloat16)).astype(jnp.float32)

@jax.custom_vjp
def low_back(v):
    return v

def low_keep(v):
    return (low(v), None)

def low_pass(kept, grad):
    return (grad,)

def back_keep(v):
    return (v, None)

def back_low(kept, grad):
    return (low(grad),)
low.defvjp(low_keep, low_pass)
low_back.defvjp(back_keep, back_low)

def both_round(operand):
    return low(low_back(operand))

def matmul(left_side, right_side):
    return jnp.dot(left_side, right_side, precision=lax.Precision.HIGHEST)

def attend(queries, key_block, value_block, seg_tree, par_tree, masked):
    row_total = queries.shape[0]
    block_rows = min(row_total, 512)
    block_count = row_total // block_rows
    query_blocks = queries.reshape(block_count, block_rows, HEADS, HEAD_DIM)
    starts = jnp.arange(block_count, dtype=jnp.int32) * block_rows
    key_heads = key_block.reshape(key_block.shape[0], HEADS, HEAD_DIM)
    value_heads = value_block.reshape(value_block.shape[0], HEADS, HEAD_DIM)
    key_pos = jnp.arange(key_block.shape[0], dtype=jnp.int32)

    @jax.checkpoint
    def one_block(block_pair):
        query_block, start = block_pair
        raw_scores = jnp.einsum('qhd,khd->hqk', query_block, key_heads, precision=lax.Precision.HIGHEST) * HEAD_DIM ** (-0.5)
        scores = low_back(raw_scores)
        if masked:
            row_pos = start + jnp.arange(block_rows, dtype=jnp.int32)
            seg_rows = lax.dynamic_slice_in_dim(seg_tree, start, block_rows)
            par_rows = lax.dynamic_slice_in_dim(par_tree, start, block_rows)
            relation = (seg_tree[None, :] == seg_rows[:, None]) | (seg_tree[None, :] == par_rows[:, None]) | (seg_tree[None, :] == 0)
            allowed = (key_pos[None, :] <= row_pos[:, None]) & relation
            scores = jnp.where(allowed[None], scores, -1e+30)
        row_top = lax.optimization_barrier(jnp.max(scores, axis=-1, keepdims=True))
        raw_weights = jnp.exp(scores - row_top)
        attn_probs = raw_weights / lax.optimization_barrier(jnp.sum(raw_weights, axis=-1, keepdims=True))
        return jnp.einsum('hqk,khd->qhd', low(attn_probs), value_heads, precision=lax.Precision.HIGHEST)
    mixed = lax.map(one_block, (query_blocks, starts))
    return mixed.reshape(row_total, HEADS * HEAD_DIM)

def tree_attention(queries, key_rows, value_rows, segment_ids, parent_ids, masked):
    tree_count = queries.shape[0] // TREE
    packed = (queries.reshape(tree_count, TREE, D), key_rows.reshape(tree_count, -1, D), value_rows.reshape(tree_count, -1, D), segment_ids.reshape(tree_count, TREE), parent_ids.reshape(tree_count, TREE))

    def one_tree(tree_group):
        return attend(tree_group[0], tree_group[1], tree_group[2], tree_group[3], tree_group[4], masked)
    return lax.map(one_tree, packed).reshape(queries.shape[0], D)

def layer(param_set, inputs_val, memory_val, teacher_val, segment_ids, parent_ids, valid_length):
    query_weight, query_bias, key_weight, value_weight, value_bias, proj_weight, proj_bias, cross_query_weight, cross_query_bias, cross_key_weight, cross_value_weight, cross_value_bias, cross_proj_weight, cross_proj_bias, up_weight, up_bias, down_weight, down_bias = param_set
    queries = both_round(matmul(inputs_val, query_weight) + query_bias)
    key_rows = both_round(matmul(inputs_val, key_weight))
    value_rows = both_round(matmul(inputs_val, value_weight) + value_bias)
    attention = both_round(tree_attention(queries, key_rows, value_rows, segment_ids, parent_ids, True))
    hidden_one = inputs_val + low_back(matmul(attention, proj_weight) + proj_bias)
    cross_queries = both_round(matmul(low(hidden_one), cross_query_weight) + cross_query_bias)
    cross_keys = both_round(matmul(memory_val, cross_key_weight))
    cross_values = both_round(matmul(memory_val, cross_value_weight) + cross_value_bias)
    cross_out = both_round(tree_attention(cross_queries, cross_keys, cross_values, segment_ids, parent_ids, False))
    hidden_two = hidden_one + low_back(matmul(cross_out, cross_proj_weight) + cross_proj_bias)
    upper = matmul(low(hidden_two), up_weight) + up_bias
    active = both_round(jnp.where(upper > 0, upper, 0.0))
    result = hidden_two + low_back(matmul(active, down_weight) + down_bias)
    positions = jnp.arange(TOKENS, dtype=jnp.int32) % TREE
    tree_of = jnp.arange(TOKENS, dtype=jnp.int32) // TREE
    valid_rows = (positions < valid_length[tree_of]).astype(result.dtype)
    count_total = jnp.sum(valid_length.astype(result.dtype))
    difference = result - teacher_val
    mean_loss = 0.5 * jnp.sum(valid_rows[:, None] * difference * difference) / count_total
    return (result, mean_loss)

def reference(inputs, memory, teacher, segment_ids, parent_ids, valid_length, query_weight, query_bias, key_weight, value_weight, value_bias, proj_weight, proj_bias, cross_query_weight, cross_query_bias, cross_key_weight, cross_value_weight, cross_value_bias, cross_proj_weight, cross_proj_bias, up_weight, up_bias, down_weight, down_bias):
    params = tuple((tensor.astype(jnp.float32) for tensor in (query_weight, query_bias, key_weight, value_weight, value_bias, proj_weight, proj_bias, cross_query_weight, cross_query_bias, cross_key_weight, cross_value_weight, cross_value_bias, cross_proj_weight, cross_proj_bias, up_weight, up_bias, down_weight, down_bias)))
    inputs_f = inputs.astype(jnp.float32)
    memory_f = memory.astype(jnp.float32)
    teacher_f = teacher.astype(jnp.float32)

    def wrapped(param_set, inputs_val, memory_val):
        return layer(param_set, inputs_val, memory_val, teacher_f, segment_ids, parent_ids, valid_length)
    (result, mean_loss), pullback = jax.vjp(wrapped, params, inputs_f, memory_f)
    grad_params, grad_input, grad_memory = pullback((jnp.zeros_like(result), jnp.ones_like(mean_loss) * TOKENS))
    return (result.astype(jnp.bfloat16), mean_loss, grad_input, grad_memory, grad_params[0], grad_params[1], grad_params[2], grad_params[3], grad_params[4], grad_params[5], grad_params[6], grad_params[7], grad_params[8], grad_params[9], grad_params[10], grad_params[11], grad_params[12], grad_params[13], grad_params[14], grad_params[15], grad_params[16], grad_params[17])
```

```python
import functools

import jax
import jax.numpy as jnp
from jax import lax
from jax.experimental import pallas as pl
from jax.experimental.pallas import tpu as pltpu
from jax.sharding import PartitionSpec as P

HEAD_DIM = 64
HEADS = 8
MASKED = -1e30
BF16 = jnp.bfloat16
F32 = jnp.float32
MESH = pl.DeviceIdType.MESH
DMA = pltpu.SemaphoreType.DMA
VMEM_LIMIT = 56 * 2**20


def mm(a, b):
    return jnp.dot(a, b, preferred_element_type=F32)


def mm_nt(a, b):
    return lax.dot_general(a, b, (((1,), (1,)), ((), ())), preferred_element_type=F32)


def mm_tn(a, b):
    return lax.dot_general(a, b, (((0,), (0,)), ((), ())), preferred_element_type=F32)


def log2_of(size):
    return size.bit_length() - 1


class Place:
    def __init__(self, rows, cols):
        self.R, self.C = rows, cols
        self.G = rows * cols
        self.half = cols // 2
        self.P = self.G // 2
        self.per_head = self.P // HEADS
        self.S = 2 * self.per_head
        self.lr, self.lc = log2_of(rows), log2_of(cols)
        self.nb = self.lr + self.lc
        self.tdim = self.lr
        self.dims = [d for d in range(self.nb) if d != self.tdim]
        self.dp = lax.axis_index("dp")
        self.row = lax.axis_index("row")
        self.col = lax.axis_index("col")
        self.core = lax.rem(self.dp, 2)
        self.tree = self.col // self.half
        self.chip = self.row * cols + self.col
        self.p = self.row * self.half + lax.rem(self.col, self.half)
        self.head = self.p // self.per_head
        self.part = lax.rem(self.p, self.per_head) * 2 + self.core
        self.bits = [lax.rem(self.row // (1 << (self.lr - 1 - i)), 2) for i in range(self.lr)] + [
            lax.rem(self.col // (1 << (self.lc - 1 - i)), 2) for i in range(self.lc)
        ]
        self.base = self.dp - self.core

    def flip(self, dims, core=False):
        row, col, dp = self.row, self.col, self.dp
        for d in dims:
            if d < self.lr:
                row = row + (1 - 2 * self.bits[d]) * (1 << (self.lr - 1 - d))
            else:
                col = col + (1 - 2 * self.bits[d]) * (1 << (self.nb - 1 - d))
        if core:
            dp = dp + 1 - 2 * self.core
        return (dp, row, col)

    def masks(self, dims):
        return [[d for i, d in enumerate(dims) if m >> i & 1] for m in range(1 << len(dims))]

    def block_of(self, head, part):
        odd = lax.rem(head, 2)
        return head * self.S + part + odd * (self.S - 1 - 2 * part)

    def block_at(self, row, col, core):
        p = row * self.half + lax.rem(col, self.half)
        return self.block_of(p // self.per_head, lax.rem(p, self.per_head) * 2 + core)

    def device_of(self, head, part):
        p = head * self.per_head + part // 2
        return (self.base + lax.rem(part, 2), p // self.half, self.tree * self.half + lax.rem(p, self.half))

    def head_xor(self, m):
        other = self.head
        for i in range(log2_of(HEADS)):
            if m >> i & 1:
                other = other + (1 - 2 * lax.rem(self.head // (1 << i), 2)) * (1 << i)
        return other


def greet_all(me):
    barrier = pltpu.get_barrier_semaphore()
    count = 0
    for mask in me.masks(list(range(me.nb))):
        for core in (False, True):
            if mask or core:
                pl.semaphore_signal(barrier, inc=1, device_id=me.flip(mask, core), device_id_type=MESH)
                count += 1
    pl.semaphore_wait(barrier, count)


def send(src, dst, send_sem, recv_sem, to):
    return pltpu.make_async_remote_copy(
        src_ref=src, dst_ref=dst, send_sem=send_sem, recv_sem=recv_sem, device_id=to, device_id_type=MESH
    )


def aligned(index, size):
    return pl.multiple_of(index * size, size)


def when_not(condition):
    return pl.when(jnp.logical_not(condition))


def gather_kernel(
    R, C, TB, units, x_ref, t_ref, w_ref, x_out, t_out, w_out,
    fs, fr, ss, rs, cs, cr, ls, ts, tr, tl, ws, wr, wl,
):
    me = Place(R, C)
    greet_all(me)
    foreign = me.core != me.tree
    U = len(units)
    masks = me.masks(me.dims)
    piece = x_ref.shape[0]

    def lanes(u):
        return pl.ds(units[u][0], units[u][1])

    def own(u):
        index = list(me.bits)
        index[me.tdim] = me.core
        return tuple(index) + (slice(None), lanes(u))

    def far(u):
        return send(
            x_ref.at[:, lanes(u)], x_out.at[tuple(me.bits) + (slice(None), lanes(u))],
            fs.at[u], fr.at[u], me.flip([me.tdim], True),
        )

    def local(u):
        return pltpu.make_async_copy(x_ref.at[:, lanes(u)], x_out.at[own(u)], ls.at[u])

    def near(u, m):
        return send(x_out.at[own(u)], x_out.at[own(u)], ss.at[u, m], rs.at[u, m], me.flip(masks[m]))

    def across(u):
        index = [slice(None)] * me.nb
        index[me.tdim] = me.core
        index = tuple(index) + (slice(None), lanes(u))
        return send(x_out.at[index], x_out.at[index], cs.at[u], cr.at[u], me.flip([], True))

    w = w_ref.shape[1]
    heads_here = w // HEAD_DIM
    w_dst = w_out.at[:, :, pl.ds(aligned(me.row, 128), 128)]
    w_jobs = []
    for t in range(2):
        for i in range(heads_here):
            for j in range(me.per_head):
                p = (me.col * heads_here + i) * me.per_head + j
                to = (me.dp, p // me.half, t * me.half + lax.rem(p, me.half))
                to_me = (to[1] == me.row) & (to[2] == me.col)
                n = len(w_jobs)
                src = w_ref.at[:, pl.ds(i * HEAD_DIM, HEAD_DIM), :]
                w_jobs.append((
                    to_me,
                    pltpu.make_async_copy(src, w_dst, wl),
                    send(src, w_dst, ws.at[n], wr.at[me.row], to),
                ))
    for to_me, here, there in w_jobs:
        pl.when(to_me)(here.start)
        when_not(to_me)(there.start)

    @pl.when(foreign)
    def _():
        for u in range(U):
            far(u).start()
        for u in range(U):
            far(u).wait()
            for m in range(1, len(masks)):
                near(u, m).start()

    @when_not(foreign)
    def _():
        for u in range(U):
            local(u).start()
        for u in range(U):
            local(u).wait()
            for m in range(1, len(masks)):
                near(u, m).start()

    t_dst = t_out.at[me.chip]

    def t_job(m, c):
        mask = masks[m]
        away = me.flip(mask)
        row = away[1]
        col = lax.rem(away[2], me.half) + me.core * me.half
        core = me.core + c * (1 - 2 * me.core)
        block = me.block_at(row, col, core)
        src = t_ref.at[:, pl.ds(aligned(block, TB), TB)]
        to_me = jnp.logical_not(foreign) & (m + c == 0)
        there = send(src, t_dst, ts.at[m, c], tr.at[m, jnp.where(foreign, 1, 0)], (me.base + core, row, col))
        return to_me, pltpu.make_async_copy(src, t_dst, tl), there

    for m in range(len(masks)):
        for c in range(2):
            to_me, here, there = t_job(m, c)
            if m + c == 0:
                pl.when(to_me)(here.start)
                when_not(to_me)(there.start)
            else:
                there.start()

    for u in range(U):
        for m in range(1, len(masks)):
            near(u, m).wait_recv()
        across(u).start()
    for r in range(R):
        from_me = (me.row == r) & (me.head // heads_here == me.col)
        got = w_out.at[:, :, pl.ds(r * 128, 128)]
        pl.when(from_me)(pltpu.make_async_copy(got, got, wl).wait)
        when_not(from_me)(send(got, got, ws.at[0], wr.at[r], me.flip([], True)).wait_recv)
    for to_me, here, there in w_jobs:
        when_not(to_me)(there.wait_send)
    for m in range(len(masks)):
        for f in range(2):
            _, here, there = t_job(m, f)
            got = send(t_ref.at[:, pl.ds(0, TB)], t_dst, ts.at[m, f], tr.at[m, f], me.flip([], True))
            if m + f == 0:
                pl.when(jnp.logical_not(foreign))(here.wait)
                pl.when(foreign)(got.wait_recv)
            else:
                got.wait_recv()
    for m in range(len(masks)):
        for c in range(2):
            to_me, here, there = t_job(m, c)
            if m + c == 0:
                when_not(to_me)(there.wait_send)
            else:
                there.wait_send()
    for u in range(U):
        for m in range(1, len(masks)):
            near(u, m).wait_send()
        across(u).wait()


def split_units(lanes, count):
    tiles = lanes // 128
    units, low = [], 0
    for i in range(count):
        width = tiles // count + (1 if i < tiles % count else 0)
        units.append((low * 128, width * 128))
        low += width
    return units


def gather_inputs(mesh_size, x_t, teacher_t, head_weights, TB):
    R, C = mesh_size
    G = R * C
    nb = log2_of(G)
    masks = G // 2
    lanes = x_t.shape[1]
    units = split_units(lanes, 5)
    U = len(units)
    w_jobs = 2 * (head_weights.shape[1] // HEAD_DIM) * (G // 2 // HEADS)
    return pl.pallas_call(
        functools.partial(gather_kernel, R, C, TB, units),
        out_shape=(
            jax.ShapeDtypeStruct((2,) * nb + (x_t.shape[0], lanes), BF16),
            jax.ShapeDtypeStruct((G, teacher_t.shape[0], TB), BF16),
            jax.ShapeDtypeStruct((3, HEAD_DIM, 128 * R), BF16),
        ),
        in_specs=[pl.BlockSpec(memory_space=pltpu.VMEM)] * 3,
        out_specs=[pl.BlockSpec(memory_space=pltpu.VMEM)] * 3,
        scratch_shapes=[
            DMA((U,)), DMA((U,)), DMA((U, masks)), DMA((U, masks)), DMA((U,)), DMA((U,)), DMA((U,)),
            DMA((masks, 2)), DMA((masks, 2)), DMA(()),
            DMA((w_jobs,)), DMA((R,)), DMA(()),
        ],
        compiler_params=pltpu.CompilerParams(
            collective_id=0, has_side_effects=True, vmem_limit_bytes=VMEM_LIMIT
        ),
    )(x_t, teacher_t, head_weights)


def heads_to_tokens(me, src_at, dst_at, sends, recvs, local):
    jobs = []
    for m in range(1, HEADS):
        other = me.head_xor(m)
        jobs.append(send(src_at(other), dst_at(me.head), sends.at[m], recvs.at[m], me.device_of(other, me.part)))
    return jobs, pltpu.make_async_copy(src_at(me.head), dst_at(me.head), local)


def to_tokens_kernel(R, C, TB, o_ref, a_out, sends, recvs, local):
    me = Place(R, C)
    greet_all(me)
    jobs, here = heads_to_tokens(
        me,
        lambda k: o_ref.at[:, pl.ds(aligned(k, TB), TB)],
        lambda h: a_out.at[pl.ds(aligned(h, HEAD_DIM), HEAD_DIM), :],
        sends, recvs, local,
    )
    for job in jobs:
        job.start()
    here.start()
    here.wait()
    for job in jobs:
        job.wait()


def to_tokens(mesh_size, o_t, TB):
    R, C = mesh_size
    return pl.pallas_call(
        functools.partial(to_tokens_kernel, R, C, TB),
        out_shape=jax.ShapeDtypeStruct((HEADS * HEAD_DIM, TB), BF16),
        in_specs=[pl.BlockSpec(memory_space=pltpu.VMEM)],
        out_specs=pl.BlockSpec(memory_space=pltpu.VMEM),
        scratch_shapes=[DMA((HEADS,)), DMA((HEADS,)), DMA(())],
        compiler_params=pltpu.CompilerParams(
            collective_id=1, has_side_effects=True, vmem_limit_bytes=VMEM_LIMIT
        ),
    )(o_t)


def blocks_to_features(me, src_ref, dst_ref, TB, piece, sends, recvs, local):
    masks = me.masks(me.dims)
    starts, waits = [], []
    dst = dst_ref.at[:, pl.ds(aligned(me.block_of(me.head, me.part), TB), TB)]
    native = me.core == me.tree
    for m, mask in enumerate(masks):
        away = me.flip(mask)
        for f in range(2):
            col = away[2]
            if f:
                col = col + (1 - 2 * me.tree) * me.half
            g = away[1] * me.C + col
            src = src_ref.at[pl.ds(aligned(g, piece), piece), :]
            there = send(src, dst, sends.at[m, f], recvs.at[m, me.core], (me.base + me.tree, away[1], col))
            got = send(src, dst, sends.at[m, f], recvs.at[m, f], me.flip([], True))
            if m + f == 0:
                here = pltpu.make_async_copy(src, dst, local)
                starts += [functools.partial(pl.when(native), here.start)]
                starts += [functools.partial(when_not(native), there.start)]
                waits += [functools.partial(pl.when(native), here.wait)]
                waits += [functools.partial(when_not(native), there.wait_send)]
            else:
                starts.append(there.start)
                waits.append(there.wait_send)
            if m == 0:
                is_local = native & (me.core == f)
                waits.append(functools.partial(when_not(is_local), got.wait_recv))
            else:
                waits.append(got.wait_recv)
    return starts, waits


def to_heads_kernel(R, C, TB, g_ref, y_ref, g_out, y_out, sends, recvs, local, ys, yr, yl):
    me = Place(R, C)
    greet_all(me)
    jobs, here = heads_to_tokens(
        me,
        lambda h: g_ref.at[pl.ds(aligned(h, HEAD_DIM), HEAD_DIM), :],
        lambda k: g_out.at[:, pl.ds(aligned(k, TB), TB)],
        sends, recvs, local,
    )
    for job in jobs:
        job.start()
    here.start()
    starts, waits = blocks_to_features(me, y_ref, y_out, TB, y_out.shape[0], ys, yr, yl)
    for start in starts:
        start()
    here.wait()
    for job in jobs:
        job.wait()
    for wait in waits:
        wait()


def to_heads(mesh_size, g_t, y_t, TB):
    R, C = mesh_size
    blocks = R * C
    features = y_t.shape[0]
    return pl.pallas_call(
        functools.partial(to_heads_kernel, R, C, TB),
        out_shape=(
            jax.ShapeDtypeStruct((HEAD_DIM, HEADS * TB), BF16),
            jax.ShapeDtypeStruct((features // blocks, blocks * TB), BF16),
        ),
        in_specs=[pl.BlockSpec(memory_space=pltpu.VMEM)] * 2,
        out_specs=[pl.BlockSpec(memory_space=pltpu.VMEM)] * 2,
        scratch_shapes=[
            DMA((HEADS,)), DMA((HEADS,)), DMA(()),
            DMA((blocks // 2, 2)), DMA((blocks // 2, 2)), DMA(()),
        ],
        compiler_params=pltpu.CompilerParams(
            collective_id=2, has_side_effects=True, vmem_limit_bytes=VMEM_LIMIT
        ),
    )(g_t, y_t)


def forward_kernel(
    R, C, TB, KC, x_ref, w_ref, b_ref, hot_ref, mask_ref,
    k_out, kt_out, v_out, q_out, o_out, of_out, lse_out, vt_ref,
):
    me = Place(R, C)
    tokens = k_out.shape[0]
    ones_row = (lax.broadcasted_iota(jnp.int32, (16, KC), 0) == 0).astype(F32)
    three_rows = (lax.broadcasted_iota(jnp.int32, (16, KC), 0) < 3).astype(F32)

    def keys(c, _):
        at = pl.ds(aligned(c, KC), KC)
        rows = mm(w_ref[pl.ds(HEAD_DIM, 2 * HEAD_DIM), :], x_ref[:, at]) + b_ref[pl.ds(HEAD_DIM, 2 * HEAD_DIM), :]
        rows = rows.astype(BF16).astype(F32)
        kt, vt = rows[:HEAD_DIM], rows[HEAD_DIM:]
        kt_out[:, at] = kt.astype(BF16)
        vt_ref[pl.ds(0, HEAD_DIM), at] = vt.astype(BF16)
        vt_ref[pl.ds(HEAD_DIM, 16), at] = ones_row.astype(BF16)
        wide = jnp.concatenate([kt, hot_ref[:, at].astype(F32), three_rows, jnp.zeros((32, KC), F32)], axis=0)
        k_out[at, :] = wide.T.astype(BF16)
        wide = jnp.concatenate([vt, three_rows, jnp.zeros((48, KC), F32)], axis=0)
        v_out[at, :] = wide.T.astype(BF16)
        return 0

    lax.fori_loop(0, tokens // KC, keys, 0)

    def block(k, _):
        index = me.block_of(k, me.part)
        at = pl.ds(aligned(index, TB), TB)
        mine = pl.ds(aligned(k, TB), TB)
        rows = mm(w_ref[pl.ds(0, HEAD_DIM), :], x_ref[:, at]) + b_ref[pl.ds(0, HEAD_DIM), :]
        rows = rows.astype(BF16).astype(F32) * HEAD_DIM ** (-0.5)
        wide = jnp.concatenate([rows, mask_ref[:, at].astype(F32), jnp.zeros((48, TB), F32)], axis=0).astype(BF16)
        q_out[:, mine] = wide

        def step(c, carry, diagonal):
            top, total = carry
            span = pl.ds(aligned(c, KC), KC)
            scores = mm(k_out[span, :], wide)
            if diagonal:
                key_pos = c * KC + lax.broadcasted_iota(jnp.int32, (KC, TB), 0)
                query_pos = index * TB + lax.broadcasted_iota(jnp.int32, (KC, TB), 1)
                scores = jnp.where(key_pos <= query_pos, scores, MASKED)
            new_top = jnp.maximum(top, jnp.max(scores, axis=0, keepdims=True))
            weights = jnp.exp(scores - new_top).astype(BF16)
            total = total * jnp.exp(top - new_top) + mm(vt_ref[:, span], weights)
            return new_top, total

        last = (index * TB) // KC
        carry = (jnp.full((1, TB), MASKED, F32), jnp.zeros((HEAD_DIM + 16, TB), F32))
        carry = lax.fori_loop(0, last, lambda c, carry: step(c, carry, False), carry)
        top, total = step(last, carry, True)
        exp_total = total[HEAD_DIM:HEAD_DIM + 1]
        mixed = total[:HEAD_DIM] / exp_total
        o_out[:, mine] = mixed.astype(BF16)
        of_out[:, mine] = mixed
        lse_out[:, mine] = jnp.broadcast_to(top + jnp.log(exp_total), (8, TB))
        return 0

    lax.fori_loop(0, HEADS, block, 0)


def forward_attention(mesh_size, x_all, w, b, hot, mask, TB, KC):
    R, C = mesh_size
    tokens = hot.shape[1]
    mine = HEADS * TB
    spec = pl.BlockSpec(memory_space=pltpu.VMEM)
    return pl.pallas_call(
        functools.partial(forward_kernel, R, C, TB, KC),
        out_shape=(
            jax.ShapeDtypeStruct((tokens, 128), BF16),
            jax.ShapeDtypeStruct((HEAD_DIM, tokens), BF16),
            jax.ShapeDtypeStruct((tokens, 128), BF16),
            jax.ShapeDtypeStruct((128, mine), BF16),
            jax.ShapeDtypeStruct((HEAD_DIM, mine), BF16),
            jax.ShapeDtypeStruct((HEAD_DIM, mine), F32),
            jax.ShapeDtypeStruct((8, mine), F32),
        ),
        in_specs=[spec] * 5,
        out_specs=[spec] * 7,
        scratch_shapes=[pltpu.VMEM((HEAD_DIM + 16, tokens), BF16)],
        compiler_params=pltpu.CompilerParams(vmem_limit_bytes=VMEM_LIMIT),
    )(x_all, w, b, hot, mask)


def three_parts(value):
    high = value.astype(BF16).astype(F32)
    rest = value - high
    middle = rest.astype(BF16).astype(F32)
    return high, middle, rest - middle


def backward_kernel(
    R, C, TB, KC, k_ref, kt_ref, v_ref, q_ref, of_ref, lse_ref, g_ref,
    dq_out, dk_out, dv_out, dk_ref, dv_ref,
):
    me = Place(R, C)
    tokens = k_ref.shape[0]
    dk_ref[...] = jnp.zeros_like(dk_ref)
    dv_ref[...] = jnp.zeros_like(dv_ref)

    def block(k, _):
        index = me.block_of(k, me.part)
        mine = pl.ds(aligned(k, TB), TB)
        grad = g_ref[:, mine]
        delta = jnp.sum(grad.astype(F32) * of_ref[:, mine], axis=0, keepdims=True)
        zeros = jnp.zeros((1, TB), F32)

        def rows(value):
            high, middle, low = three_parts(-value)
            return jnp.concatenate([high, middle, low] + [zeros] * 13, axis=0).astype(BF16)

        query = q_ref[pl.ds(0, HEAD_DIM), mine]
        wide_q = jnp.concatenate(
            [q_ref[pl.ds(0, HEAD_DIM + 16), mine], rows(lse_ref[pl.ds(0, 1), mine]), jnp.zeros((32, TB), BF16)], axis=0
        )
        wide_g = jnp.concatenate([grad, rows(delta), jnp.zeros((48, TB), BF16)], axis=0)

        def step(c, dq, diagonal):
            span = pl.ds(aligned(c, KC), KC)
            probs = jnp.exp(mm(k_ref[span, :], wide_q))
            if diagonal:
                key_pos = c * KC + lax.broadcasted_iota(jnp.int32, (KC, TB), 0)
                query_pos = index * TB + lax.broadcasted_iota(jnp.int32, (KC, TB), 1)
                probs = jnp.where(key_pos <= query_pos, probs, 0.0)
            dscores = (probs * mm(v_ref[span, :], wide_g)).astype(BF16)
            dv_ref[:, span] += mm_nt(grad, probs.astype(BF16))
            dk_ref[:, span] += mm_nt(query, dscores)
            return dq + mm(kt_ref[:, span], dscores)

        last = (index * TB) // KC
        dq = lax.fori_loop(0, last, lambda c, dq: step(c, dq, False), jnp.zeros((HEAD_DIM, TB), F32))
        dq = step(last, dq, True)
        dq_out[:, mine] = (dq * HEAD_DIM ** (-0.5)).astype(BF16)
        return 0

    lax.fori_loop(0, HEADS, block, 0)
    dk_out[...] = dk_ref[...].astype(BF16)
    dv_out[...] = dv_ref[...].astype(BF16)


def backward_attention(mesh_size, k, kt, v, q, of, lse, g, TB, KC):
    R, C = mesh_size
    tokens = k.shape[0]
    spec = pl.BlockSpec(memory_space=pltpu.VMEM)
    return pl.pallas_call(
        functools.partial(backward_kernel, R, C, TB, KC),
        out_shape=(
            jax.ShapeDtypeStruct((HEAD_DIM, HEADS * TB), BF16),
            jax.ShapeDtypeStruct((HEAD_DIM, tokens), BF16),
            jax.ShapeDtypeStruct((HEAD_DIM, tokens), BF16),
        ),
        in_specs=[spec] * 7,
        out_specs=[spec] * 3,
        scratch_shapes=[pltpu.VMEM((HEAD_DIM, tokens), F32)] * 2,
        compiler_params=pltpu.CompilerParams(vmem_limit_bytes=VMEM_LIMIT),
    )(k, kt, v, q, of, lse, g)


def grads_kernel(
    R, C, TB, dq_ref, dk_ref, dv_ref, dw_ref, d_out, kv_out, w_out, part_buf,
    ps, pr, sends, recvs, local, ws, wr, wl,
):
    me = Place(R, C)
    greet_all(me)
    heads_here = (HEADS * HEAD_DIM // C) // HEAD_DIM
    per_head = me.per_head

    w_jobs = []
    for r in range(R):
        to = (me.dp, r, me.head // heads_here)
        to_me = (me.row == r) & (to[2] == me.col)
        slot = me.tree * per_head + lax.rem(me.p, per_head)
        src = dw_ref.at[:, :, pl.ds(r * 128, 128)]
        dst = w_out.at[lax.rem(me.head, heads_here), slot]
        w_jobs.append((
            to_me,
            pltpu.make_async_copy(src, dst, wl),
            send(src, dst, ws.at[r], wr.at[lax.rem(me.head, heads_here), slot], to),
        ))

    p_jobs = []
    for j in range(1, me.S):
        other = lax.rem(me.part + j, me.S)
        for k in range(HEADS):
            src_at = pl.ds(aligned(me.block_of(k, other), TB), TB)
            for i, ref in enumerate((dk_ref, dv_ref)):
                p_jobs.append(send(
                    ref.at[:, src_at], part_buf.at[j - 1, i, :, pl.ds(k * TB, TB)],
                    ps.at[j - 1, i, k], pr.at[j - 1, i, k], me.device_of(me.head, other),
                ))
    for job in p_jobs:
        job.start()
    jobs, here = heads_to_tokens(
        me,
        lambda k: dq_ref.at[:, pl.ds(aligned(k, TB), TB)],
        lambda h: d_out.at[0, pl.ds(aligned(h, HEAD_DIM), HEAD_DIM), :],
        sends.at[0], recvs.at[0], local.at[0],
    )
    heres = [here]
    for job in jobs:
        job.start()
    here.start()
    for job in p_jobs:
        job.wait()
    for i, ref in enumerate((dk_ref, dv_ref)):
        for k in range(HEADS):
            total = ref[:, pl.ds(aligned(me.block_of(k, me.part), TB), TB)].astype(F32)
            for j in range(1, me.S):
                total += part_buf[j - 1, i, :, pl.ds(k * TB, TB)].astype(F32)
            kv_out[i, :, pl.ds(k * TB, TB)] = total.astype(BF16)
    for i in range(2):
        more, here = heads_to_tokens(
            me,
            lambda k: kv_out.at[i, :, pl.ds(aligned(k, TB), TB)],
            lambda h: d_out.at[1 + i, pl.ds(aligned(h, HEAD_DIM), HEAD_DIM), :],
            sends.at[1 + i], recvs.at[1 + i], local.at[1 + i],
        )
        for job in more:
            job.start()
        here.start()
        jobs += more
        heres.append(here)
    for to_me, here, there in w_jobs:
        pl.when(to_me)(here.start)
        when_not(to_me)(there.start)
    for here in heres:
        here.wait()
    for job in jobs:
        job.wait()
    for to_me, here, there in w_jobs:
        pl.when(to_me)(here.wait)
        when_not(to_me)(there.wait_send)
    for i in range(heads_here):
        for t in range(2):
            for j in range(per_head):
                p = (me.col * heads_here + i) * per_head + j
                row, col = p // me.half, t * me.half + lax.rem(p, me.half)
                from_me = (row == me.row) & (col == me.col)
                slot = t * per_head + j
                got = w_out.at[i, slot]
                when_not(from_me)(send(got, got, ws.at[0], wr.at[i, slot], me.flip([], True)).wait_recv)


def grads_home(mesh_size, dq, dk, dv, dw, TB):
    R, C = mesh_size
    per_head = R * C // 2 // HEADS
    S = 2 * per_head
    heads_here = HEADS // C
    return pl.pallas_call(
        functools.partial(grads_kernel, R, C, TB),
        out_shape=(
            jax.ShapeDtypeStruct((3, HEADS * HEAD_DIM, TB), BF16),
            jax.ShapeDtypeStruct((2, HEAD_DIM, HEADS * TB), BF16),
            jax.ShapeDtypeStruct((heads_here, 2 * per_head, 3, HEAD_DIM, 128), BF16),
        ),
        in_specs=[pl.BlockSpec(memory_space=pltpu.VMEM)] * 4,
        out_specs=[pl.BlockSpec(memory_space=pltpu.VMEM)] * 3,
        scratch_shapes=[
            pltpu.VMEM((S - 1, 2, HEAD_DIM, HEADS * TB), BF16),
            DMA((S - 1, 2, HEADS)), DMA((S - 1, 2, HEADS)),
            DMA((3, HEADS)), DMA((3, HEADS)), DMA((3,)),
            DMA((R,)), DMA((heads_here, 2 * per_head)), DMA(()),
        ],
        compiler_params=pltpu.CompilerParams(
            collective_id=3, has_side_effects=True, vmem_limit_bytes=VMEM_LIMIT
        ),
    )(dq, dk, dv, dw)


def features_kernel(R, C, TB, y_ref, y_out, ys, yr, yl):
    me = Place(R, C)
    greet_all(me)
    starts, waits = blocks_to_features(me, y_ref, y_out, TB, y_out.shape[0], ys, yr, yl)
    for start in starts:
        start()
    for wait in waits:
        wait()


def to_features(mesh_size, y_t, TB):
    R, C = mesh_size
    blocks = R * C
    return pl.pallas_call(
        functools.partial(features_kernel, R, C, TB),
        out_shape=jax.ShapeDtypeStruct((y_t.shape[0] // blocks, blocks * TB), y_t.dtype),
        in_specs=[pl.BlockSpec(memory_space=pltpu.VMEM)],
        out_specs=pl.BlockSpec(memory_space=pltpu.VMEM),
        scratch_shapes=[DMA((blocks // 2, 2)), DMA((blocks // 2, 2)), DMA(())],
        compiler_params=pltpu.CompilerParams(
            collective_id=4, has_side_effects=True, vmem_limit_bytes=VMEM_LIMIT
        ),
    )(y_t)


def column_sums(operand):
    return jnp.sum(operand.astype(F32), axis=0)


def shards(
    R, C,
    inputs, memory, teacher, segment_ids, parent_ids, valid_length,
    query_weight, query_bias, key_weight, value_weight, value_bias, proj_weight, proj_bias,
    cross_query_weight, cross_query_bias, cross_key_weight, cross_value_weight, cross_value_bias,
    cross_proj_weight, cross_proj_bias, up_weight, up_bias, down_weight, down_bias,
):
    mesh_size = (R, C)
    me = Place(R, C)
    G = R * C
    tokens = inputs.shape[0]
    mem_rows = memory.shape[0]
    TB = tokens // G
    KC = 512
    w = query_weight.shape[1]
    D = inputs.shape[1] * G
    pairs = lax.axis_size("dp")
    swap = [(i, i ^ 1) for i in range(pairs)]
    native = me.core == me.tree

    ids = jnp.stack([segment_ids, parent_ids])
    ids = jnp.where(native, ids, lax.ppermute(ids, "dp", swap))
    lengths = lax.all_gather(valid_length[0], "dp")
    my_length = lengths[me.base + me.tree]
    count_total = jnp.sum(lengths).astype(F32)
    segment = jnp.arange(16, dtype=jnp.int32)[:, None]
    hot = (ids[0][None] == segment).astype(BF16)
    seen = (segment == ids[0][None]) | (segment == ids[1][None]) | (segment == 0)
    mask = jnp.where(seen, 0.0, MASKED).astype(BF16)

    head_weights = jnp.stack([query_weight.T, key_weight.T, value_weight.T])
    x_t = jnp.concatenate([inputs.T, memory.T], axis=1)
    x_all, teacher_all, w_head = gather_inputs(mesh_size, x_t, teacher.T, head_weights, TB)
    x_all = x_all.reshape(D, tokens + mem_rows)
    teacher_mine = teacher_all.reshape(D, TB).T.astype(F32)
    w_head = w_head.reshape(3 * HEAD_DIM, D)

    across = jnp.concatenate(
        [query_weight, key_weight, value_weight, cross_query_weight, cross_key_weight, cross_value_weight, up_weight],
        axis=1,
    )
    along = jnp.concatenate([proj_weight, cross_proj_weight, down_weight], axis=0)
    across_all = lax.all_gather(across, ("row", "col")).reshape(R, C, across.shape[0], across.shape[1])
    along_all = lax.all_gather(along, ("row", "col")).reshape(R, C, along.shape[0], along.shape[1])

    def across_part(low, width):
        return across_all[:, :, :, low * w:(low + width) * w].transpose(0, 2, 1, 3).reshape(D, width * w * C)

    def along_part(low, width):
        return along_all[:, :, low * w:(low + width) * w].transpose(1, 2, 0, 3).reshape(width * w * C, D)

    Wq, Wk, Wv, Wcq, Wck, Wcv = [across_part(i, 1) for i in range(6)]
    Wup = across_part(6, 4)
    Wproj, Wcproj, Wdown = along_part(0, 1), along_part(1, 1), along_part(2, 4)
    biases = jnp.concatenate([
        query_bias, value_bias, cross_query_bias, cross_value_bias, up_bias, proj_bias, cross_proj_bias, down_bias
    ])
    biases = lax.all_gather(biases, ("row", "col")).astype(F32).reshape(R, C, -1)

    def col_bias(low, width):
        return biases[0, :, low * w:(low + width) * w].reshape(-1)

    def row_bias(index):
        low = 8 * w + index * (D // R)
        return biases[:, 0, low:low + D // R].reshape(-1)

    b_q, b_v, b_cq, b_cv = [col_bias(i, 1) for i in range(4)]
    b_up = col_bias(4, 4)
    b_proj, b_cproj, b_down = [row_bias(i) for i in range(3)]

    def head_slice(vector):
        return lax.dynamic_slice_in_dim(vector, me.head * HEAD_DIM, HEAD_DIM)

    b_head = jnp.concatenate([head_slice(b_q), jnp.zeros((HEAD_DIM,), F32), head_slice(b_v)])[:, None]

    k, kt, v, q, o, of, lse = forward_attention(mesh_size, x_all, w_head, b_head, hot, mask, TB, KC)
    attention = to_tokens(mesh_size, o, TB).T

    block = me.block_of(me.head, me.part)
    x_mine = lax.dynamic_slice_in_dim(x_all, block * TB, TB, axis=1).T
    mem = x_all[:, tokens:].T
    hidden_one = x_mine.astype(F32) + (mm(attention, Wproj) + b_proj)
    hidden_one_b = hidden_one.astype(BF16)
    cross_q = (mm(hidden_one_b, Wcq) + b_cq).astype(BF16)
    cross_k = mm(mem, Wck).astype(BF16)
    cross_v = (mm(mem, Wcv) + b_cv).astype(BF16)

    def heads_of(operand):
        return operand.reshape(operand.shape[0], HEADS, HEAD_DIM)

    scale = HEAD_DIM ** (-0.5)
    scores = jnp.einsum("qhd,khd->hkq", heads_of(cross_q), heads_of(cross_k), preferred_element_type=F32) * scale
    raw = jnp.exp(scores - jnp.max(scores, axis=1, keepdims=True))
    probs = raw / jnp.sum(raw, axis=1, keepdims=True)
    probs_b = probs.astype(BF16)
    cross_out = jnp.einsum(
        "hkq,khd->qhd", probs_b, heads_of(cross_v), preferred_element_type=F32
    ).reshape(TB, D).astype(BF16)
    hidden_two = hidden_one + (mm(cross_out, Wcproj) + b_cproj)
    hidden_two_b = hidden_two.astype(BF16)
    upper = mm(hidden_two_b, Wup) + b_up
    active = jnp.where(upper > 0, upper, 0.0).astype(BF16)
    result = hidden_two + (mm(active, Wdown) + b_down)
    output = result.astype(BF16)
    position = block * TB + jnp.arange(TB, dtype=jnp.int32)
    valid = (position < my_length).astype(F32)[:, None]
    difference = result - teacher_mine
    square_part = jnp.sum(valid * difference * difference)
    grad_result = float(pairs * tokens) / count_total * valid * difference
    grad_out = grad_result.astype(BF16)
    g_down = mm_tn(active, grad_out)
    grad_upper = jnp.where(upper > 0, mm_nt(grad_out, Wdown), 0.0).astype(BF16)
    g_up = mm_tn(hidden_two_b, grad_upper)
    grad_two = grad_result + mm_nt(grad_upper, Wup)
    grad_cross = grad_two.astype(BF16)
    g_cproj = mm_tn(cross_out, grad_cross)
    grad_cross_out = mm_nt(grad_cross, Wcproj).astype(BF16)
    grad_probs = jnp.einsum(
        "qhd,khd->hkq", heads_of(grad_cross_out), heads_of(cross_v), preferred_element_type=F32
    )
    delta = jnp.sum(grad_probs * probs, axis=1, keepdims=True)
    grad_scores = (probs * (grad_probs - delta)).astype(BF16)
    grad_cq = (
        jnp.einsum("hkq,khd->qhd", grad_scores, heads_of(cross_k), preferred_element_type=F32) * scale
    ).reshape(TB, D).astype(BF16)
    grad_ck = (
        jnp.einsum("hkq,qhd->khd", grad_scores, heads_of(cross_q), preferred_element_type=F32) * scale
    ).reshape(mem_rows, D).astype(BF16)
    grad_cv = jnp.einsum(
        "hkq,qhd->khd", probs_b, heads_of(grad_cross_out), preferred_element_type=F32
    ).reshape(mem_rows, D).astype(BF16)
    g_cq = mm_tn(hidden_one_b, grad_cq)
    g_ck = mm_tn(mem, grad_ck)
    g_cv = mm_tn(mem, grad_cv)
    memory_part = (mm_nt(grad_ck, Wck) + mm_nt(grad_cv, Wcv)).astype(BF16)
    grad_one = grad_two + mm_nt(grad_cq, Wcq)
    grad_branch = grad_one.astype(BF16)
    g_proj = mm_tn(attention, grad_branch)
    grad_attention = mm_nt(grad_branch, Wproj).astype(BF16)

    grad_heads, output_t = to_heads(mesh_size, grad_attention.T, output.T, TB)
    dq, dk, dv = backward_attention(mesh_size, k, kt, v, q, of, lse, grad_heads, TB, KC)
    mine = jnp.concatenate([
        lax.dynamic_slice_in_dim(x_all, me.block_of(i, me.part) * TB, TB, axis=1) for i in range(HEADS)
    ], axis=1)
    dw = jnp.stack([mm_nt(dq, mine), mm_nt(dk, x_all[:, :tokens]), mm_nt(dv, x_all[:, :tokens])]).astype(BF16)
    d_tokens, kv_tokens, dw_parts = grads_home(mesh_size, dq, dk, dv, dw, TB)
    bias_q = jnp.sum(dq.astype(F32), axis=1)
    bias_v = jnp.sum(kv_tokens[1].astype(F32), axis=1)
    grad_input = grad_one + mm_tn(d_tokens[0], Wq.T) + mm_tn(d_tokens[1], Wk.T) + mm_tn(d_tokens[2], Wv.T)
    grad_input_t = to_features(mesh_size, grad_input.T.astype(BF16), TB)

    dw_sum = jnp.sum(dw_parts.astype(F32), axis=1)
    dw_sum = dw_sum.transpose(1, 3, 0, 2).reshape(3, D // R, w)

    def across_grad(value):
        return value.astype(BF16).reshape(R, D // R, C, -1).transpose(0, 2, 1, 3).reshape(G, D // R, -1)

    def along_grad(value):
        return value.astype(BF16).reshape(C, -1, R, D // R).transpose(2, 0, 1, 3).reshape(G, -1, D // R)

    across_g = jnp.concatenate([across_grad(g) for g in (g_cq, g_ck, g_cv, g_up)], axis=2)
    along_g = jnp.concatenate([along_grad(g) for g in (g_proj, g_cproj, g_down)], axis=1)
    across_g = lax.psum_scatter(across_g, ("row", "col"), scatter_dimension=0, tiled=True)[0]
    along_g = lax.psum_scatter(along_g, ("row", "col"), scatter_dimension=0, tiled=True)[0]
    memory_sum = lax.psum_scatter(
        jnp.where(me.tree == jnp.arange(2)[:, None, None], memory_part.T[None], 0), "dp", scatter_dimension=0, tiled=True
    ) if pairs == 2 else None
    if pairs != 2:
        both = jnp.where(me.tree == jnp.arange(2)[:, None, None], memory_part.T[None], 0).astype(BF16)
        swapped = lax.ppermute(both, "dp", swap)
        memory_sum = lax.dynamic_slice_in_dim(both + swapped, me.core, 1, axis=0)
    grad_memory = lax.psum_scatter(memory_sum[0], ("row", "col"), scatter_dimension=0, tiled=True)
    place = [jnp.zeros((HEADS, HEAD_DIM), F32).at[me.head].set(b).reshape(-1) for b in (bias_q, bias_v)]
    small = jnp.concatenate(place + [
        column_sums(grad_cq), column_sums(grad_cv), column_sums(grad_upper),
        column_sums(grad_branch), column_sums(grad_cross), column_sums(grad_out), square_part[None],
    ])
    small = lax.psum(small, ("dp", "row", "col"))
    mean_loss = 0.5 * small[-1] / count_total
    low = 0
    vectors = []
    for i, width in enumerate((D, D, D, D, 4 * D, D, D, D)):
        piece = width // (C if i < 5 else R)
        at = low + piece * (me.col if i < 5 else me.row)
        vectors.append(lax.dynamic_slice_in_dim(small, at, piece))
        low += width
    dw_sum, across_g, along_g = [
        lax.psum(g.astype(BF16), "dp").astype(F32) for g in (dw_sum, across_g, along_g)
    ]
    return (
        output_t.T, mean_loss, grad_input_t.T.astype(F32), grad_memory.T.astype(F32),
        dw_sum[0], vectors[0], dw_sum[1], dw_sum[2], vectors[1],
        along_g[:w], vectors[5],
        across_g[:, :w], vectors[2], across_g[:, w:2 * w], across_g[:, 2 * w:3 * w], vectors[3],
        along_g[w:2 * w], vectors[6],
        across_g[:, 3 * w:], vectors[4],
        along_g[2 * w:], vectors[7],
    )


def solution(mesh):
    col, row, both = P("row", "col"), P("col", "row"), P("dp", ("row", "col"))
    in_specs = (
        both, both, both, P("dp"), P("dp"), P("dp"),
        col, P("col"), col, col, P("col"), row, P("row"),
        col, P("col"), col, col, P("col"), row, P("row"),
        col, P("col"), row, P("row"),
    )
    out_specs = (
        both, P(), both, both,
        col, P("col"), col, col, P("col"), row, P("row"),
        col, P("col"), col, col, P("col"), row, P("row"),
        col, P("col"), row, P("row"),
    )
    body = functools.partial(shards, mesh.shape["row"], mesh.shape["col"])
    return jax.shard_map(body, mesh=mesh, in_specs=in_specs, out_specs=out_specs, check_vma=False)
```

```python
import functools

import jax
import jax.numpy as jnp
from jax import lax
from jax.experimental import pallas as pl
from jax.experimental.pallas import tpu as pltpu
from jax.sharding import PartitionSpec as P

HEAD_DIM = 64
HEADS = 8
MASKED = -1e30
BF16 = jnp.bfloat16
F32 = jnp.float32
MESH = pl.DeviceIdType.MESH
DMA = pltpu.SemaphoreType.DMA
VMEM_LIMIT = 56 * 2**20


def mm(a, b):
    return jnp.dot(a, b, preferred_element_type=F32)


def mm_nt(a, b):
    return lax.dot_general(a, b, (((1,), (1,)), ((), ())), preferred_element_type=F32)


def mm_tn(a, b):
    return lax.dot_general(a, b, (((0,), (0,)), ((), ())), preferred_element_type=F32)


def log2_of(size):
    return size.bit_length() - 1


class Place:
    def __init__(self, rows, cols):
        self.R, self.C = rows, cols
        self.G = rows * cols
        self.half = cols // 2
        self.P = self.G // 2
        self.per_head = self.P // HEADS
        self.S = 2 * self.per_head
        self.lr, self.lc = log2_of(rows), log2_of(cols)
        self.nb = self.lr + self.lc
        self.tdim = self.lr
        self.dims = [d for d in range(self.nb) if d != self.tdim]
        self.dp = lax.axis_index("dp")
        self.row = lax.axis_index("row")
        self.col = lax.axis_index("col")
        self.core = lax.rem(self.dp, 2)
        self.tree = self.col // self.half
        self.chip = self.row * cols + self.col
        self.p = self.row * self.half + lax.rem(self.col, self.half)
        self.head = self.p // self.per_head
        self.part = lax.rem(self.p, self.per_head) * 2 + self.core
        self.bits = [lax.rem(self.row // (1 << (self.lr - 1 - i)), 2) for i in range(self.lr)] + [
            lax.rem(self.col // (1 << (self.lc - 1 - i)), 2) for i in range(self.lc)
        ]
        self.base = self.dp - self.core

    def flip(self, dims, core=False):
        row, col, dp = self.row, self.col, self.dp
        for d in dims:
            if d < self.lr:
                row = row + (1 - 2 * self.bits[d]) * (1 << (self.lr - 1 - d))
            else:
                col = col + (1 - 2 * self.bits[d]) * (1 << (self.nb - 1 - d))
        if core:
            dp = dp + 1 - 2 * self.core
        return (dp, row, col)

    def masks(self, dims):
        return [[d for i, d in enumerate(dims) if m >> i & 1] for m in range(1 << len(dims))]

    def block_of(self, head, part):
        odd = lax.rem(head, 2)
        return head * self.S + part + odd * (self.S - 1 - 2 * part)

    def block_at(self, row, col, core):
        p = row * self.half + lax.rem(col, self.half)
        return self.block_of(p // self.per_head, lax.rem(p, self.per_head) * 2 + core)

    def device_of(self, head, part):
        p = head * self.per_head + part // 2
        return (self.base + lax.rem(part, 2), p // self.half, self.tree * self.half + lax.rem(p, self.half))

    def head_xor(self, m):
        other = self.head
        for i in range(log2_of(HEADS)):
            if m >> i & 1:
                other = other + (1 - 2 * lax.rem(self.head // (1 << i), 2)) * (1 << i)
        return other


def greet_all(me):
    barrier = pltpu.get_barrier_semaphore()
    count = 0
    for mask in me.masks(list(range(me.nb))):
        for core in (False, True):
            if mask or core:
                pl.semaphore_signal(barrier, inc=1, device_id=me.flip(mask, core), device_id_type=MESH)
                count += 1
    pl.semaphore_wait(barrier, count)


def send(src, dst, send_sem, recv_sem, to):
    return pltpu.make_async_remote_copy(
        src_ref=src, dst_ref=dst, send_sem=send_sem, recv_sem=recv_sem, device_id=to, device_id_type=MESH
    )


def aligned(index, size):
    return pl.multiple_of(index * size, size)


def when_not(condition):
    return pl.when(jnp.logical_not(condition))


def gather_kernel(
    R, C, TB, units, x_ref, t_ref, w_ref, x_out, t_out, w_out,
    fs, fr, ss, rs, cs, cr, ls, ts, tr, tl, ws, wr, wl,
):
    me = Place(R, C)
    greet_all(me)
    foreign = me.core != me.tree
    U = len(units)
    masks = me.masks(me.dims)
    piece = x_ref.shape[0]

    def lanes(u):
        return pl.ds(units[u][0], units[u][1])

    def own(u):
        index = list(me.bits)
        index[me.tdim] = me.core
        return tuple(index) + (slice(None), lanes(u))

    def far(u):
        return send(
            x_ref.at[:, lanes(u)], x_out.at[tuple(me.bits) + (slice(None), lanes(u))],
            fs.at[u], fr.at[u], me.flip([me.tdim], True),
        )

    def local(u):
        return pltpu.make_async_copy(x_ref.at[:, lanes(u)], x_out.at[own(u)], ls.at[u])

    def near(u, m):
        return send(x_out.at[own(u)], x_out.at[own(u)], ss.at[u, m], rs.at[u, m], me.flip(masks[m]))

    def across(u):
        index = [slice(None)] * me.nb
        index[me.tdim] = me.core
        index = tuple(index) + (slice(None), lanes(u))
        return send(x_out.at[index], x_out.at[index], cs.at[u], cr.at[u], me.flip([], True))

    w = w_ref.shape[1]
    heads_here = w // HEAD_DIM
    w_dst = w_out.at[:, :, pl.ds(aligned(me.row, 128), 128)]
    w_jobs = []
    for t in range(2):
        for i in range(heads_here):
            for j in range(me.per_head):
                p = (me.col * heads_here + i) * me.per_head + j
                to = (me.dp, p // me.half, t * me.half + lax.rem(p, me.half))
                to_me = (to[1] == me.row) & (to[2] == me.col)
                n = len(w_jobs)
                src = w_ref.at[:, pl.ds(i * HEAD_DIM, HEAD_DIM), :]
                w_jobs.append((
                    to_me,
                    pltpu.make_async_copy(src, w_dst, wl),
                    send(src, w_dst, ws.at[n], wr.at[me.row], to),
                ))
    for to_me, here, there in w_jobs:
        pl.when(to_me)(here.start)
        when_not(to_me)(there.start)

    @pl.when(foreign)
    def _():
        for u in range(U):
            far(u).start()
        for u in range(U):
            far(u).wait()
            for m in range(1, len(masks)):
                near(u, m).start()

    @when_not(foreign)
    def _():
        for u in range(U):
            local(u).start()
        for u in range(U):
            local(u).wait()
            for m in range(1, len(masks)):
                near(u, m).start()

    t_dst = t_out.at[me.chip]

    def t_job(m, c):
        mask = masks[m]
        away = me.flip(mask)
        row = away[1]
        col = lax.rem(away[2], me.half) + me.core * me.half
        core = me.core + c * (1 - 2 * me.core)
        block = me.block_at(row, col, core)
        src = t_ref.at[:, pl.ds(aligned(block, TB), TB)]
        to_me = jnp.logical_not(foreign) & (m + c == 0)
        there = send(src, t_dst, ts.at[m, c], tr.at[m, jnp.where(foreign, 1, 0)], (me.base + core, row, col))
        return to_me, pltpu.make_async_copy(src, t_dst, tl), there

    for m in range(len(masks)):
        for c in range(2):
            to_me, here, there = t_job(m, c)
            if m + c == 0:
                pl.when(to_me)(here.start)
                when_not(to_me)(there.start)
            else:
                there.start()

    for u in range(U):
        for m in range(1, len(masks)):
            near(u, m).wait_recv()
        across(u).start()
    for r in range(R):
        from_me = (me.row == r) & (me.head // heads_here == me.col)
        got = w_out.at[:, :, pl.ds(r * 128, 128)]
        pl.when(from_me)(pltpu.make_async_copy(got, got, wl).wait)
        when_not(from_me)(send(got, got, ws.at[0], wr.at[r], me.flip([], True)).wait_recv)
    for to_me, here, there in w_jobs:
        when_not(to_me)(there.wait_send)
    for m in range(len(masks)):
        for f in range(2):
            _, here, there = t_job(m, f)
            got = send(t_ref.at[:, pl.ds(0, TB)], t_dst, ts.at[m, f], tr.at[m, f], me.flip([], True))
            if m + f == 0:
                pl.when(jnp.logical_not(foreign))(here.wait)
                pl.when(foreign)(got.wait_recv)
            else:
                got.wait_recv()
    for m in range(len(masks)):
        for c in range(2):
            to_me, here, there = t_job(m, c)
            if m + c == 0:
                when_not(to_me)(there.wait_send)
            else:
                there.wait_send()
    for u in range(U):
        for m in range(1, len(masks)):
            near(u, m).wait_send()
        across(u).wait()


def split_units(lanes, count):
    tiles = lanes // 128
    units, low = [], 0
    for i in range(count):
        width = tiles // count + (1 if i < tiles % count else 0)
        units.append((low * 128, width * 128))
        low += width
    return units


def gather_inputs(mesh_size, x_t, teacher_t, head_weights, TB):
    R, C = mesh_size
    G = R * C
    nb = log2_of(G)
    masks = G // 2
    lanes = x_t.shape[1]
    units = split_units(lanes, 5)
    U = len(units)
    w_jobs = 2 * (head_weights.shape[1] // HEAD_DIM) * (G // 2 // HEADS)
    return pl.pallas_call(
        functools.partial(gather_kernel, R, C, TB, units),
        out_shape=(
            jax.ShapeDtypeStruct((2,) * nb + (x_t.shape[0], lanes), BF16),
            jax.ShapeDtypeStruct((G, teacher_t.shape[0], TB), BF16),
            jax.ShapeDtypeStruct((3, HEAD_DIM, 128 * R), BF16),
        ),
        in_specs=[pl.BlockSpec(memory_space=pltpu.VMEM)] * 3,
        out_specs=[pl.BlockSpec(memory_space=pltpu.VMEM)] * 3,
        scratch_shapes=[
            DMA((U,)), DMA((U,)), DMA((U, masks)), DMA((U, masks)), DMA((U,)), DMA((U,)), DMA((U,)),
            DMA((masks, 2)), DMA((masks, 2)), DMA(()),
            DMA((w_jobs,)), DMA((R,)), DMA(()),
        ],
        compiler_params=pltpu.CompilerParams(
            collective_id=0, has_side_effects=True, vmem_limit_bytes=VMEM_LIMIT
        ),
    )(x_t, teacher_t, head_weights)


def heads_to_tokens(me, src_at, dst_at, sends, recvs, local):
    jobs = []
    for m in range(1, HEADS):
        other = me.head_xor(m)
        jobs.append(send(src_at(other), dst_at(me.head), sends.at[m], recvs.at[m], me.device_of(other, me.part)))
    return jobs, pltpu.make_async_copy(src_at(me.head), dst_at(me.head), local)


def to_tokens_kernel(R, C, TB, o_ref, a_out, sends, recvs, local):
    me = Place(R, C)
    greet_all(me)
    jobs, here = heads_to_tokens(
        me,
        lambda k: o_ref.at[:, pl.ds(aligned(k, TB), TB)],
        lambda h: a_out.at[pl.ds(aligned(h, HEAD_DIM), HEAD_DIM), :],
        sends, recvs, local,
    )
    for job in jobs:
        job.start()
    here.start()
    here.wait()
    for job in jobs:
        job.wait()


def to_tokens(mesh_size, o_t, TB):
    R, C = mesh_size
    return pl.pallas_call(
        functools.partial(to_tokens_kernel, R, C, TB),
        out_shape=jax.ShapeDtypeStruct((HEADS * HEAD_DIM, TB), BF16),
        in_specs=[pl.BlockSpec(memory_space=pltpu.VMEM)],
        out_specs=pl.BlockSpec(memory_space=pltpu.VMEM),
        scratch_shapes=[DMA((HEADS,)), DMA((HEADS,)), DMA(())],
        compiler_params=pltpu.CompilerParams(
            collective_id=1, has_side_effects=True, vmem_limit_bytes=VMEM_LIMIT
        ),
    )(o_t)


def blocks_to_features(me, src_ref, dst_ref, TB, piece, sends, recvs, local):
    masks = me.masks(me.dims)
    starts, waits = [], []
    dst = dst_ref.at[:, pl.ds(aligned(me.block_of(me.head, me.part), TB), TB)]
    native = me.core == me.tree
    for m, mask in enumerate(masks):
        away = me.flip(mask)
        for f in range(2):
            col = away[2]
            if f:
                col = col + (1 - 2 * me.tree) * me.half
            g = away[1] * me.C + col
            src = src_ref.at[pl.ds(aligned(g, piece), piece), :]
            there = send(src, dst, sends.at[m, f], recvs.at[m, me.core], (me.base + me.tree, away[1], col))
            got = send(src, dst, sends.at[m, f], recvs.at[m, f], me.flip([], True))
            if m + f == 0:
                here = pltpu.make_async_copy(src, dst, local)
                starts += [functools.partial(pl.when(native), here.start)]
                starts += [functools.partial(when_not(native), there.start)]
                waits += [functools.partial(pl.when(native), here.wait)]
                waits += [functools.partial(when_not(native), there.wait_send)]
            else:
                starts.append(there.start)
                waits.append(there.wait_send)
            if m == 0:
                is_local = native & (me.core == f)
                waits.append(functools.partial(when_not(is_local), got.wait_recv))
            else:
                waits.append(got.wait_recv)
    return starts, waits


def to_heads_kernel(R, C, TB, g_ref, y_ref, g_out, y_out, sends, recvs, local, ys, yr, yl):
    me = Place(R, C)
    greet_all(me)
    jobs, here = heads_to_tokens(
        me,
        lambda h: g_ref.at[pl.ds(aligned(h, HEAD_DIM), HEAD_DIM), :],
        lambda k: g_out.at[:, pl.ds(aligned(k, TB), TB)],
        sends, recvs, local,
    )
    for job in jobs:
        job.start()
    here.start()
    starts, waits = blocks_to_features(me, y_ref, y_out, TB, y_out.shape[0], ys, yr, yl)
    for start in starts:
        start()
    here.wait()
    for job in jobs:
        job.wait()
    for wait in waits:
        wait()


def to_heads(mesh_size, g_t, y_t, TB):
    R, C = mesh_size
    blocks = R * C
    features = y_t.shape[0]
    return pl.pallas_call(
        functools.partial(to_heads_kernel, R, C, TB),
        out_shape=(
            jax.ShapeDtypeStruct((HEAD_DIM, HEADS * TB), BF16),
            jax.ShapeDtypeStruct((features // blocks, blocks * TB), BF16),
        ),
        in_specs=[pl.BlockSpec(memory_space=pltpu.VMEM)] * 2,
        out_specs=[pl.BlockSpec(memory_space=pltpu.VMEM)] * 2,
        scratch_shapes=[
            DMA((HEADS,)), DMA((HEADS,)), DMA(()),
            DMA((blocks // 2, 2)), DMA((blocks // 2, 2)), DMA(()),
        ],
        compiler_params=pltpu.CompilerParams(
            collective_id=2, has_side_effects=True, vmem_limit_bytes=VMEM_LIMIT
        ),
    )(g_t, y_t)


def forward_kernel(
    R, C, TB, KC, x_ref, w_ref, b_ref, hot_ref, mask_ref,
    k_out, kt_out, v_out, q_out, o_out, of_out, lse_out, vt_ref,
):
    me = Place(R, C)
    tokens = k_out.shape[0]
    ones_row = (lax.broadcasted_iota(jnp.int32, (16, KC), 0) == 0).astype(F32)
    three_rows = (lax.broadcasted_iota(jnp.int32, (16, KC), 0) < 3).astype(F32)

    def keys(c, _):
        at = pl.ds(aligned(c, KC), KC)
        rows = mm(w_ref[pl.ds(HEAD_DIM, 2 * HEAD_DIM), :], x_ref[:, at]) + b_ref[pl.ds(HEAD_DIM, 2 * HEAD_DIM), :]
        rows = rows.astype(BF16).astype(F32)
        kt, vt = rows[:HEAD_DIM], rows[HEAD_DIM:]
        kt_out[:, at] = kt.astype(BF16)
        vt_ref[pl.ds(0, HEAD_DIM), at] = vt.astype(BF16)
        vt_ref[pl.ds(HEAD_DIM, 16), at] = ones_row.astype(BF16)
        wide = jnp.concatenate([kt, hot_ref[:, at].astype(F32), three_rows, jnp.zeros((32, KC), F32)], axis=0)
        k_out[at, :] = wide.T.astype(BF16)
        wide = jnp.concatenate([vt, three_rows, jnp.zeros((48, KC), F32)], axis=0)
        v_out[at, :] = wide.T.astype(BF16)
        return 0

    lax.fori_loop(0, tokens // KC, keys, 0)

    def block(k, _):
        index = me.block_of(k, me.part)
        at = pl.ds(aligned(index, TB), TB)
        mine = pl.ds(aligned(k, TB), TB)
        rows = mm(w_ref[pl.ds(0, HEAD_DIM), :], x_ref[:, at]) + b_ref[pl.ds(0, HEAD_DIM), :]
        rows = rows.astype(BF16).astype(F32) * HEAD_DIM ** (-0.5)
        wide = jnp.concatenate([rows, mask_ref[:, at].astype(F32), jnp.zeros((48, TB), F32)], axis=0).astype(BF16)
        q_out[:, mine] = wide

        def step(c, carry, diagonal):
            top, total = carry
            span = pl.ds(aligned(c, KC), KC)
            scores = mm(k_out[span, :], wide)
            if diagonal:
                key_pos = c * KC + lax.broadcasted_iota(jnp.int32, (KC, TB), 0)
                query_pos = index * TB + lax.broadcasted_iota(jnp.int32, (KC, TB), 1)
                scores = jnp.where(key_pos <= query_pos, scores, MASKED)
            new_top = jnp.maximum(top, jnp.max(scores, axis=0, keepdims=True))
            weights = jnp.exp(scores - new_top).astype(BF16)
            total = total * jnp.exp(top - new_top) + mm(vt_ref[:, span], weights)
            return new_top, total

        last = (index * TB) // KC
        carry = (jnp.full((1, TB), MASKED, F32), jnp.zeros((HEAD_DIM + 16, TB), F32))
        carry = lax.fori_loop(0, last, lambda c, carry: step(c, carry, False), carry)
        top, total = step(last, carry, True)
        exp_total = total[HEAD_DIM:HEAD_DIM + 1]
        mixed = total[:HEAD_DIM] / exp_total
        o_out[:, mine] = mixed.astype(BF16)
        of_out[:, mine] = mixed
        lse_out[:, mine] = jnp.broadcast_to(top + jnp.log(exp_total), (8, TB))
        return 0

    lax.fori_loop(0, HEADS, block, 0)


def forward_attention(mesh_size, x_all, w, b, hot, mask, TB, KC):
    R, C = mesh_size
    tokens = hot.shape[1]
    mine = HEADS * TB
    spec = pl.BlockSpec(memory_space=pltpu.VMEM)
    return pl.pallas_call(
        functools.partial(forward_kernel, R, C, TB, KC),
        out_shape=(
            jax.ShapeDtypeStruct((tokens, 128), BF16),
            jax.ShapeDtypeStruct((HEAD_DIM, tokens), BF16),
            jax.ShapeDtypeStruct((tokens, 128), BF16),
            jax.ShapeDtypeStruct((128, mine), BF16),
            jax.ShapeDtypeStruct((HEAD_DIM, mine), BF16),
            jax.ShapeDtypeStruct((HEAD_DIM, mine), F32),
            jax.ShapeDtypeStruct((8, mine), F32),
        ),
        in_specs=[spec] * 5,
        out_specs=[spec] * 7,
        scratch_shapes=[pltpu.VMEM((HEAD_DIM + 16, tokens), BF16)],
        compiler_params=pltpu.CompilerParams(vmem_limit_bytes=VMEM_LIMIT),
    )(x_all, w, b, hot, mask)


def three_parts(value):
    high = value.astype(BF16).astype(F32)
    rest = value - high
    middle = rest.astype(BF16).astype(F32)
    return high, middle, rest - middle


def backward_kernel(
    R, C, TB, KC, k_ref, kt_ref, v_ref, q_ref, of_ref, lse_ref, g_ref,
    dq_out, dk_out, dv_out, dk_ref, dv_ref,
):
    me = Place(R, C)
    tokens = k_ref.shape[0]
    dk_ref[...] = jnp.zeros_like(dk_ref)
    dv_ref[...] = jnp.zeros_like(dv_ref)

    def block(k, _):
        index = me.block_of(k, me.part)
        mine = pl.ds(aligned(k, TB), TB)
        grad = g_ref[:, mine]
        delta = jnp.sum(grad.astype(F32) * of_ref[:, mine], axis=0, keepdims=True)
        zeros = jnp.zeros((1, TB), F32)

        def rows(value):
            high, middle, low = three_parts(-value)
            return jnp.concatenate([high, middle, low] + [zeros] * 13, axis=0).astype(BF16)

        query = q_ref[pl.ds(0, HEAD_DIM), mine]
        wide_q = jnp.concatenate(
            [q_ref[pl.ds(0, HEAD_DIM + 16), mine], rows(lse_ref[pl.ds(0, 1), mine]), jnp.zeros((32, TB), BF16)], axis=0
        )
        wide_g = jnp.concatenate([grad, rows(delta), jnp.zeros((48, TB), BF16)], axis=0)

        def step(c, dq, diagonal):
            span = pl.ds(aligned(c, KC), KC)
            probs = jnp.exp(mm(k_ref[span, :], wide_q))
            if diagonal:
                key_pos = c * KC + lax.broadcasted_iota(jnp.int32, (KC, TB), 0)
                query_pos = index * TB + lax.broadcasted_iota(jnp.int32, (KC, TB), 1)
                probs = jnp.where(key_pos <= query_pos, probs, 0.0)
            dscores = (probs * mm(v_ref[span, :], wide_g)).astype(BF16)
            dv_ref[:, span] += mm_nt(grad, probs.astype(BF16))
            dk_ref[:, span] += mm_nt(query, dscores)
            return dq + mm(kt_ref[:, span], dscores)

        last = (index * TB) // KC
        dq = lax.fori_loop(0, last, lambda c, dq: step(c, dq, False), jnp.zeros((HEAD_DIM, TB), F32))
        dq = step(last, dq, True)
        dq_out[:, mine] = (dq * HEAD_DIM ** (-0.5)).astype(BF16)
        return 0

    lax.fori_loop(0, HEADS, block, 0)
    dk_out[...] = dk_ref[...].astype(BF16)
    dv_out[...] = dv_ref[...].astype(BF16)


def backward_attention(mesh_size, k, kt, v, q, of, lse, g, TB, KC):
    R, C = mesh_size
    tokens = k.shape[0]
    spec = pl.BlockSpec(memory_space=pltpu.VMEM)
    return pl.pallas_call(
        functools.partial(backward_kernel, R, C, TB, KC),
        out_shape=(
            jax.ShapeDtypeStruct((HEAD_DIM, HEADS * TB), BF16),
            jax.ShapeDtypeStruct((HEAD_DIM, tokens), BF16),
            jax.ShapeDtypeStruct((HEAD_DIM, tokens), BF16),
        ),
        in_specs=[spec] * 7,
        out_specs=[spec] * 3,
        scratch_shapes=[pltpu.VMEM((HEAD_DIM, tokens), F32)] * 2,
        compiler_params=pltpu.CompilerParams(vmem_limit_bytes=VMEM_LIMIT),
    )(k, kt, v, q, of, lse, g)


def grads_kernel(
    R, C, TB, dq_ref, dk_ref, dv_ref, dw_ref, d_out, kv_out, w_out, part_buf,
    ps, pr, sends, recvs, local, ws, wr, wl,
):
    me = Place(R, C)
    greet_all(me)
    heads_here = (HEADS * HEAD_DIM // C) // HEAD_DIM
    per_head = me.per_head

    w_jobs = []
    for r in range(R):
        to = (me.dp, r, me.head // heads_here)
        to_me = (me.row == r) & (to[2] == me.col)
        slot = me.tree * per_head + lax.rem(me.p, per_head)
        src = dw_ref.at[:, :, pl.ds(r * 128, 128)]
        dst = w_out.at[lax.rem(me.head, heads_here), slot]
        w_jobs.append((
            to_me,
            pltpu.make_async_copy(src, dst, wl),
            send(src, dst, ws.at[r], wr.at[lax.rem(me.head, heads_here), slot], to),
        ))

    p_jobs = []
    for j in range(1, me.S):
        other = lax.rem(me.part + j, me.S)
        for k in range(HEADS):
            src_at = pl.ds(aligned(me.block_of(k, other), TB), TB)
            for i, ref in enumerate((dk_ref, dv_ref)):
                p_jobs.append(send(
                    ref.at[:, src_at], part_buf.at[j - 1, i, :, pl.ds(k * TB, TB)],
                    ps.at[j - 1, i, k], pr.at[j - 1, i, k], me.device_of(me.head, other),
                ))
    for job in p_jobs:
        job.start()
    jobs, here = heads_to_tokens(
        me,
        lambda k: dq_ref.at[:, pl.ds(aligned(k, TB), TB)],
        lambda h: d_out.at[0, pl.ds(aligned(h, HEAD_DIM), HEAD_DIM), :],
        sends.at[0], recvs.at[0], local.at[0],
    )
    heres = [here]
    for job in jobs:
        job.start()
    here.start()
    for job in p_jobs:
        job.wait()
    for i, ref in enumerate((dk_ref, dv_ref)):
        for k in range(HEADS):
            total = ref[:, pl.ds(aligned(me.block_of(k, me.part), TB), TB)].astype(F32)
            for j in range(1, me.S):
                total += part_buf[j - 1, i, :, pl.ds(k * TB, TB)].astype(F32)
            kv_out[i, :, pl.ds(k * TB, TB)] = total.astype(BF16)
    for i in range(2):
        more, here = heads_to_tokens(
            me,
            lambda k: kv_out.at[i, :, pl.ds(aligned(k, TB), TB)],
            lambda h: d_out.at[1 + i, pl.ds(aligned(h, HEAD_DIM), HEAD_DIM), :],
            sends.at[1 + i], recvs.at[1 + i], local.at[1 + i],
        )
        for job in more:
            job.start()
        here.start()
        jobs += more
        heres.append(here)
    for to_me, here, there in w_jobs:
        pl.when(to_me)(here.start)
        when_not(to_me)(there.start)
    for here in heres:
        here.wait()
    for job in jobs:
        job.wait()
    for to_me, here, there in w_jobs:
        pl.when(to_me)(here.wait)
        when_not(to_me)(there.wait_send)
    for i in range(heads_here):
        for t in range(2):
            for j in range(per_head):
                p = (me.col * heads_here + i) * per_head + j
                row, col = p // me.half, t * me.half + lax.rem(p, me.half)
                from_me = (row == me.row) & (col == me.col)
                slot = t * per_head + j
                got = w_out.at[i, slot]
                when_not(from_me)(send(got, got, ws.at[0], wr.at[i, slot], me.flip([], True)).wait_recv)


def grads_home(mesh_size, dq, dk, dv, dw, TB):
    R, C = mesh_size
    per_head = R * C // 2 // HEADS
    S = 2 * per_head
    heads_here = HEADS // C
    return pl.pallas_call(
        functools.partial(grads_kernel, R, C, TB),
        out_shape=(
            jax.ShapeDtypeStruct((3, HEADS * HEAD_DIM, TB), BF16),
            jax.ShapeDtypeStruct((2, HEAD_DIM, HEADS * TB), BF16),
            jax.ShapeDtypeStruct((heads_here, 2 * per_head, 3, HEAD_DIM, 128), BF16),
        ),
        in_specs=[pl.BlockSpec(memory_space=pltpu.VMEM)] * 4,
        out_specs=[pl.BlockSpec(memory_space=pltpu.VMEM)] * 3,
        scratch_shapes=[
            pltpu.VMEM((S - 1, 2, HEAD_DIM, HEADS * TB), BF16),
            DMA((S - 1, 2, HEADS)), DMA((S - 1, 2, HEADS)),
            DMA((3, HEADS)), DMA((3, HEADS)), DMA((3,)),
            DMA((R,)), DMA((heads_here, 2 * per_head)), DMA(()),
        ],
        compiler_params=pltpu.CompilerParams(
            collective_id=3, has_side_effects=True, vmem_limit_bytes=VMEM_LIMIT
        ),
    )(dq, dk, dv, dw)


def features_kernel(R, C, TB, y_ref, y_out, ys, yr, yl):
    me = Place(R, C)
    greet_all(me)
    starts, waits = blocks_to_features(me, y_ref, y_out, TB, y_out.shape[0], ys, yr, yl)
    for start in starts:
        start()
    for wait in waits:
        wait()


def to_features(mesh_size, y_t, TB):
    R, C = mesh_size
    blocks = R * C
    return pl.pallas_call(
        functools.partial(features_kernel, R, C, TB),
        out_shape=jax.ShapeDtypeStruct((y_t.shape[0] // blocks, blocks * TB), y_t.dtype),
        in_specs=[pl.BlockSpec(memory_space=pltpu.VMEM)],
        out_specs=pl.BlockSpec(memory_space=pltpu.VMEM),
        scratch_shapes=[DMA((blocks // 2, 2)), DMA((blocks // 2, 2)), DMA(())],
        compiler_params=pltpu.CompilerParams(
            collective_id=4, has_side_effects=True, vmem_limit_bytes=VMEM_LIMIT
        ),
    )(y_t)


def flipped(value):
    return value.astype(F32).T


def token_kernel(
    R, C, at_ref, x_ref, teacher_ref, across_ref, along_ref, rows_ref, up_row_ref, valid_ref, factor_ref, mine_ref,
    ga_out, y_out, one_out, across_out, along_out, mem_out, rows_out, up_row_out,
    wcq, wck, wcv, wup, wproj, wcproj, wdown, ck, cv, ckt, cvt, probs_ref, ot_ref, q_ref, g_ref, dqt_ref, dck, dcv,
):
    TB = at_ref.shape[1]
    D = at_ref.shape[0]
    rows_r = D // R
    w = D // C
    mem_rows = ck.shape[0]
    tokens = x_ref.shape[1] - mem_rows
    scale = HEAD_DIM ** (-0.5)

    def gather_across(dst, low, width):
        for r in range(R):
            dst[pl.ds(r * rows_r, rows_r), :] = jnp.concatenate(
                [across_ref[r * C + c, :, pl.ds(low * w, width * w)] for c in range(C)], axis=1
            )

    def gather_along(dst, low, width):
        for c in range(C):
            dst[pl.ds(c * width * w, width * w), :] = jnp.concatenate(
                [along_ref[r * C + c, pl.ds(low * w, width * w), :] for r in range(R)], axis=1
            )

    gather_along(wproj, 0, 1)
    gather_across(wcq, 3, 1)
    gather_across(wck, 4, 1)
    gather_across(wcv, 5, 1)
    gather_along(wcproj, 1, 1)
    gather_across(wup, 6, 4)
    gather_along(wdown, 2, 4)

    b_cq, b_cv, b_proj, b_cproj, b_down = [rows_ref[pl.ds(i, 1), :] for i in range(5)]

    mem_t = x_ref[:, pl.ds(tokens, mem_rows)]
    mem = flipped(mem_t).astype(BF16)
    ck[...] = mm(mem, wck[...]).astype(BF16)
    cv[...] = (mm(mem, wcv[...]) + b_cv).astype(BF16)
    ckt[...] = flipped(ck[...]).astype(BF16)
    cvt[...] = flipped(cv[...]).astype(BF16)

    attention = flipped(at_ref[...]).astype(BF16)
    x_mine = flipped(mine_ref[...])
    hidden_one = x_mine + (mm(attention, wproj[...]) + b_proj)
    hidden_one_b = hidden_one.astype(BF16)
    q_ref[...] = (mm(hidden_one_b, wcq[...]) + b_cq).astype(BF16)

    lane = lax.broadcasted_iota(jnp.int32, (TB, 128), 1)

    def halves(value):
        zero = jnp.zeros_like(value)
        return [jnp.where((lane < HEAD_DIM) if i == 0 else (lane >= HEAD_DIM), value, zero) for i in range(2)]

    def cross_forward(pair, _):
        at = pl.ds(aligned(pair, 128), 128)
        query = halves((q_ref[:, at].astype(F32) * scale).astype(BF16))
        for i in range(2):
            scores = mm_nt(ck[:, at], query[i])
            raw = jnp.exp(scores - jnp.max(scores, axis=0, keepdims=True))
            probs = (raw * (1.0 / jnp.sum(raw, axis=0, keepdims=True))).astype(BF16)
            probs_ref[pair * 2 + i] = probs
            head = pl.ds(aligned(pair * 2 + i, HEAD_DIM), HEAD_DIM)
            ot_ref[head, :] = mm(cvt[head, :], probs)
        return 0

    lax.fori_loop(0, HEADS // 2, cross_forward, 0)
    cross_out = ot_ref[...].T.astype(BF16)
    hidden_two = hidden_one + (mm(cross_out, wcproj[...]) + b_cproj)
    hidden_two_b = hidden_two.astype(BF16)
    active = jnp.maximum(mm(hidden_two_b, wup[...]) + up_row_ref[...], 0.0).astype(BF16)
    result = hidden_two + (mm(active, wdown[...]) + b_down)
    y_out[...] = result.T.astype(BF16)
    difference = (result - flipped(teacher_ref[...])) * valid_ref[...]
    rows_out[pl.ds(5, 1), :] = jnp.sum(difference * difference, axis=0, keepdims=True)
    grad_result = factor_ref[...] * difference
    grad_out = grad_result.astype(BF16)

    def sums(value):
        return jnp.sum(value.astype(F32), axis=0, keepdims=True)

    def put_along(low, width, left, right):
        for c in range(C):
            part = mm_tn(left[:, c * width * w:(c + 1) * width * w], right).astype(BF16)
            for r in range(R):
                along_out[r * C + c, pl.ds(low * w, width * w), :] = part[:, r * rows_r:(r + 1) * rows_r]

    def put_across(low, width, left, right):
        for r in range(R):
            part = mm_tn(left[:, r * rows_r:(r + 1) * rows_r], right).astype(BF16)
            for c in range(C):
                across_out[r * C + c, :, pl.ds(low * w, width * w)] = part[:, c * width * w:(c + 1) * width * w]

    rows_out[pl.ds(4, 1), :] = sums(grad_out)
    put_along(2, 4, active, grad_out)
    grad_active = mm_nt(grad_out, wdown[...])
    grad_upper = jnp.where(active > 0, grad_active, 0.0).astype(BF16)
    up_row_out[...] = sums(grad_upper)
    put_across(3, 4, hidden_two_b, grad_upper)
    grad_two = grad_result + mm_nt(grad_upper, wup[...])
    grad_cross = grad_two.astype(BF16)
    rows_out[pl.ds(3, 1), :] = sums(grad_cross)
    put_along(1, 1, cross_out, grad_cross)
    grad_cross_out = mm_nt(grad_cross, wcproj[...]).astype(BF16)
    g_ref[...] = grad_cross_out
    ot_ref[...] = ot_ref[...] * flipped(grad_cross_out)

    def cross_backward(pair, _):
        at = pl.ds(aligned(pair, 128), 128)
        query = halves((q_ref[:, at].astype(F32) * scale).astype(BF16))
        grad = halves(g_ref[:, at])
        dk = jnp.zeros((mem_rows, 128), F32)
        dv = jnp.zeros((mem_rows, 128), F32)
        for i in range(2):
            head = pl.ds(aligned(pair * 2 + i, HEAD_DIM), HEAD_DIM)
            delta = jnp.sum(ot_ref[head, :], axis=0, keepdims=True)
            probs = probs_ref[pair * 2 + i]
            dprobs = mm_nt(cv[:, at], grad[i])
            dscores = (probs.astype(F32) * (dprobs - delta)).astype(BF16)
            dqt_ref[head, :] = mm(ckt[head, :], dscores) * scale
            dk += mm(dscores, query[i])
            dv += mm(probs, grad[i])
        dck[:, at] = dk.astype(BF16)
        dcv[:, at] = dv.astype(BF16)
        return 0

    lax.fori_loop(0, HEADS // 2, cross_backward, 0)
    grad_cq = dqt_ref[...].T.astype(BF16)
    rows_out[pl.ds(0, 1), :] = sums(grad_cq)
    rows_out[pl.ds(1, 1), :] = sums(dcv[...])
    put_across(0, 1, hidden_one_b, grad_cq)
    put_across(1, 1, mem, dck[...])
    put_across(2, 1, mem, dcv[...])
    mem_out[...] = (mm_nt(wck[...], dck[...]) + mm_nt(wcv[...], dcv[...])).astype(BF16)
    grad_one = grad_two + mm_nt(grad_cq, wcq[...])
    one_out[...] = grad_one
    grad_branch = grad_one.astype(BF16)
    rows_out[pl.ds(2, 1), :] = sums(grad_branch)
    put_along(0, 1, attention, grad_branch)
    ga_out[...] = mm_nt(wproj[...], grad_branch).astype(BF16)


def token_block(mesh_size, at, x_all, teacher, across_all, along_all, rows, up_row, valid, factor, x_mine):
    R, C = mesh_size
    D, TB = at.shape
    G = R * C
    w = D // C
    tokens = TB * G
    mem_rows = x_all.shape[1] - tokens
    FF = 4 * D
    spec = pl.BlockSpec(memory_space=pltpu.VMEM)
    return pl.pallas_call(
        functools.partial(token_kernel, R, C),
        out_shape=(
            jax.ShapeDtypeStruct((D, TB), BF16),
            jax.ShapeDtypeStruct((D, TB), BF16),
            jax.ShapeDtypeStruct((TB, D), F32),
            jax.ShapeDtypeStruct((G, D // R, 7 * w), BF16),
            jax.ShapeDtypeStruct((G, 6 * w, D // R), BF16),
            jax.ShapeDtypeStruct((D, mem_rows), BF16),
            jax.ShapeDtypeStruct((8, D), F32),
            jax.ShapeDtypeStruct((1, FF), F32),
        ),
        in_specs=[spec] * 10,
        out_specs=[spec] * 8,
        scratch_shapes=[
            pltpu.VMEM((D, D), BF16), pltpu.VMEM((D, D), BF16), pltpu.VMEM((D, D), BF16), pltpu.VMEM((D, FF), BF16),
            pltpu.VMEM((D, D), BF16), pltpu.VMEM((D, D), BF16), pltpu.VMEM((FF, D), BF16),
            pltpu.VMEM((mem_rows, D), BF16), pltpu.VMEM((mem_rows, D), BF16),
            pltpu.VMEM((D, mem_rows), BF16), pltpu.VMEM((D, mem_rows), BF16),
            pltpu.VMEM((HEADS, mem_rows, TB), BF16),
            pltpu.VMEM((D, TB), F32), pltpu.VMEM((TB, D), BF16), pltpu.VMEM((TB, D), BF16), pltpu.VMEM((D, TB), F32),
            pltpu.VMEM((mem_rows, D), BF16), pltpu.VMEM((mem_rows, D), BF16),
        ],
        compiler_params=pltpu.CompilerParams(vmem_limit_bytes=VMEM_LIMIT),
    )(at, x_all, teacher, across_all, along_all, rows, up_row, valid, factor, x_mine)


def shards(
    R, C,
    inputs, memory, teacher, segment_ids, parent_ids, valid_length,
    query_weight, query_bias, key_weight, value_weight, value_bias, proj_weight, proj_bias,
    cross_query_weight, cross_query_bias, cross_key_weight, cross_value_weight, cross_value_bias,
    cross_proj_weight, cross_proj_bias, up_weight, up_bias, down_weight, down_bias,
):
    mesh_size = (R, C)
    me = Place(R, C)
    G = R * C
    tokens = inputs.shape[0]
    mem_rows = memory.shape[0]
    TB = tokens // G
    KC = 512
    w = query_weight.shape[1]
    D = inputs.shape[1] * G
    pairs = lax.axis_size("dp")
    swap = [(i, i ^ 1) for i in range(pairs)]
    native = me.core == me.tree

    ids = jnp.stack([segment_ids, parent_ids])
    ids = jnp.where(native, ids, lax.ppermute(ids, "dp", swap))
    lengths = lax.all_gather(valid_length[0], "dp")
    my_length = lengths[me.base + me.tree]
    count_total = jnp.sum(lengths).astype(F32)
    segment = jnp.arange(16, dtype=jnp.int32)[:, None]
    hot = (ids[0][None] == segment).astype(BF16)
    seen = (segment == ids[0][None]) | (segment == ids[1][None]) | (segment == 0)
    mask = jnp.where(seen, 0.0, MASKED).astype(BF16)

    head_weights = jnp.stack([query_weight.T, key_weight.T, value_weight.T])
    x_t = jnp.concatenate([inputs.T, memory.T], axis=1)
    x_all, teacher_all, w_head = gather_inputs(mesh_size, x_t, teacher.T, head_weights, TB)
    x_all = x_all.reshape(D, tokens + mem_rows)
    w_head = w_head.reshape(3 * HEAD_DIM, D)

    across = jnp.concatenate(
        [query_weight, key_weight, value_weight, cross_query_weight, cross_key_weight, cross_value_weight, up_weight],
        axis=1,
    )
    along = jnp.concatenate([proj_weight, cross_proj_weight, down_weight], axis=0)
    across_all = lax.all_gather(across, ("row", "col")).reshape(R, C, across.shape[0], across.shape[1])
    along_all = lax.all_gather(along, ("row", "col")).reshape(R, C, along.shape[0], along.shape[1])

    def across_part(low, width):
        return across_all[:, :, :, low * w:(low + width) * w].transpose(0, 2, 1, 3).reshape(D, width * w * C)

    Wq, Wk, Wv = [across_part(i, 1) for i in range(3)]
    biases = jnp.concatenate([
        query_bias, value_bias, cross_query_bias, cross_value_bias, up_bias, proj_bias, cross_proj_bias, down_bias
    ])
    biases = lax.all_gather(biases, ("row", "col")).astype(F32).reshape(R, C, -1)

    def col_bias(low, width):
        return biases[0, :, low * w:(low + width) * w].reshape(-1)

    def row_bias(index):
        low = 8 * w + index * (D // R)
        return biases[:, 0, low:low + D // R].reshape(-1)

    b_q, b_v, b_cq, b_cv = [col_bias(i, 1) for i in range(4)]
    b_up = col_bias(4, 4)
    b_proj, b_cproj, b_down = [row_bias(i) for i in range(3)]

    def head_slice(vector):
        return lax.dynamic_slice_in_dim(vector, me.head * HEAD_DIM, HEAD_DIM)

    b_head = jnp.concatenate([head_slice(b_q), jnp.zeros((HEAD_DIM,), F32), head_slice(b_v)])[:, None]

    k, kt, v, q, o, of, lse = forward_attention(mesh_size, x_all, w_head, b_head, hot, mask, TB, KC)
    attention_t = to_tokens(mesh_size, o, TB)

    block = me.block_of(me.head, me.part)
    x_mine = lax.dynamic_slice_in_dim(x_all, block * TB, TB, axis=1)
    position = block * TB + jnp.arange(TB, dtype=jnp.int32)
    valid = (position < my_length).astype(F32)[:, None]
    factor = (float(pairs * tokens) / count_total).reshape(1, 1)
    rows = jnp.stack([b_cq, b_cv, b_proj, b_cproj, b_down] + [jnp.zeros((D,), F32)] * 3)
    grad_attention_t, output_mine, grad_one, across_g, along_g, memory_part, row_sums, up_sums = token_block(
        mesh_size, attention_t, x_all, teacher_all.reshape(D, TB), across_all.reshape(G, D // R, -1),
        along_all.reshape(G, -1, D // R), rows, b_up[None], valid, factor, x_mine,
    )

    grad_heads, output_t = to_heads(mesh_size, grad_attention_t, output_mine, TB)
    dq, dk, dv = backward_attention(mesh_size, k, kt, v, q, of, lse, grad_heads, TB, KC)
    mine = jnp.concatenate([
        lax.dynamic_slice_in_dim(x_all, me.block_of(i, me.part) * TB, TB, axis=1) for i in range(HEADS)
    ], axis=1)
    dw = jnp.stack([mm_nt(dq, mine), mm_nt(dk, x_all[:, :tokens]), mm_nt(dv, x_all[:, :tokens])]).astype(BF16)
    d_tokens, kv_tokens, dw_parts = grads_home(mesh_size, dq, dk, dv, dw, TB)
    bias_q = jnp.sum(dq.astype(F32), axis=1)
    bias_v = jnp.sum(kv_tokens[1].astype(F32), axis=1)
    grad_input = grad_one + mm_tn(d_tokens[0], Wq.T) + mm_tn(d_tokens[1], Wk.T) + mm_tn(d_tokens[2], Wv.T)
    grad_input_t = to_features(mesh_size, grad_input.T.astype(BF16), TB)

    dw_sum = jnp.sum(dw_parts.astype(F32), axis=1)
    dw_sum = dw_sum.transpose(1, 3, 0, 2).reshape(3, D // R, w)

    across_g = lax.psum_scatter(across_g, ("row", "col"), scatter_dimension=0, tiled=True)[0]
    along_g = lax.psum_scatter(along_g, ("row", "col"), scatter_dimension=0, tiled=True)[0]
    memory_sum = lax.psum_scatter(
        jnp.where(me.tree == jnp.arange(2)[:, None, None], memory_part[None], 0), "dp", scatter_dimension=0, tiled=True
    ) if pairs == 2 else None
    if pairs != 2:
        both = jnp.where(me.tree == jnp.arange(2)[:, None, None], memory_part[None], 0).astype(BF16)
        swapped = lax.ppermute(both, "dp", swap)
        memory_sum = lax.dynamic_slice_in_dim(both + swapped, me.core, 1, axis=0)
    grad_memory = lax.psum_scatter(memory_sum[0], ("row", "col"), scatter_dimension=0, tiled=True)
    place = [jnp.zeros((HEADS, HEAD_DIM), F32).at[me.head].set(b).reshape(-1) for b in (bias_q, bias_v)]
    small = jnp.concatenate(place + [
        row_sums[0], row_sums[1], up_sums[0], row_sums[2], row_sums[3], row_sums[4], jnp.sum(row_sums[5])[None],
    ])
    small = lax.psum(small, ("dp", "row", "col"))
    mean_loss = 0.5 * small[-1] / count_total
    low = 0
    vectors = []
    for i, width in enumerate((D, D, D, D, 4 * D, D, D, D)):
        piece = width // (C if i < 5 else R)
        at = low + piece * (me.col if i < 5 else me.row)
        vectors.append(lax.dynamic_slice_in_dim(small, at, piece))
        low += width
    dw_sum, across_g, along_g = [
        lax.psum(g.astype(BF16), "dp").astype(F32) for g in (dw_sum, across_g, along_g)
    ]
    return (
        output_t.T, mean_loss, grad_input_t.T.astype(F32), grad_memory.T.astype(F32),
        dw_sum[0], vectors[0], dw_sum[1], dw_sum[2], vectors[1],
        along_g[:w], vectors[5],
        across_g[:, :w], vectors[2], across_g[:, w:2 * w], across_g[:, 2 * w:3 * w], vectors[3],
        along_g[w:2 * w], vectors[6],
        across_g[:, 3 * w:], vectors[4],
        along_g[2 * w:], vectors[7],
    )


def solution(mesh):
    col, row, both = P("row", "col"), P("col", "row"), P("dp", ("row", "col"))
    in_specs = (
        both, both, both, P("dp"), P("dp"), P("dp"),
        col, P("col"), col, col, P("col"), row, P("row"),
        col, P("col"), col, col, P("col"), row, P("row"),
        col, P("col"), row, P("row"),
    )
    out_specs = (
        both, P(), both, both,
        col, P("col"), col, col, P("col"), row, P("row"),
        col, P("col"), col, col, P("col"), row, P("row"),
        col, P("col"), row, P("row"),
    )
    body = functools.partial(shards, mesh.shape["row"], mesh.shape["col"])
    return jax.shard_map(body, mesh=mesh, in_specs=in_specs, out_specs=out_specs, check_vma=False)
```
